512 devices in a mesh: dom: 512 (over x, y, z, core).
Axes of the slice: x: 4, y: 4, z: 16, core: 2. Of those that a mesh axis runs over, the one named last changes fastest.
Arguments:
- source: float32 [4, 4, 20, 65536], P(None, None, None, 'dom'), may hold values from -6 to 6
- absorption: float32 [4, 65536], P(None, 'dom'), may hold values from 0.5 to 4
- geometry: float32 [3, 65536], P(None, 'dom'), may hold values from 0.2 to 0.6
- penalty: float32 [4, 65536], P(None, 'dom'), may hold values from 0.5 to 4.5
- face_link: int32 [4, 65536], P(None, 'dom'), may hold values from 0 to 768, as said below
- face_orient: int32 [4, 65536], P(None, 'dom'), may hold values from 0 to 5
- send_index: int32 [512, 8, 32], P('dom'), may hold values from 0 to 512, as said below
- live_count: int32 [512], P('dom'), may hold values from 64 to 128, as said below
- mass_matrix: float32 [20, 20], replicated, as said below
- stiffness: float32 [3, 20, 20], replicated, may hold values from -1.25 to 1.25
Outputs:
- solution: float32 [4, 4, 20, 65536], P(None, None, None, 'dom')
- residual: float32 [4, 4, 20, 65536], P(None, None, None, 'dom')
The draws below stay inside these ranges and needn't reach their ends.
Inputs may be any that keep to these rules, and one draw needn't show every extreme that they name: `face_link`: values below 512 name a local trace f * 128 + local element; values from 512 name received slot q * 32 + s; the largest value means a boundary face. `send_index`: the value 4 * 128 marks an empty slot. `live_count`: some partition is full in every draw. `mass_matrix`: Symmetric, unit diagonal, off-diagonal entries of magnitude at most 0.04.
All inputs are finite; a program needn't handle non-finite values.
Results may differ from the reference program's by a relative error of at most 0.0003.
Values sent between devices are 32-bit elements; how exact they have to be, the bound alone decides.
A program may use at most 64 MiB of HBM per device.

```python
import math
import jax
import jax.numpy as jnp
import numpy as np
from jax import lax

GASES = 4
COMPS = 4
NODES = 20
FACES = 4
REACH = 4
ITERS = 2
E_DEV = 128
SLOTS = 32
PEERS = 8
ELEMS = 65536
N_DOM = 512


def draw_penalty(key, part):
    device = (jnp.arange(ELEMS) // E_DEV).astype(jnp.float32)
    ramp = 1.0 + 2.0 * device / max(N_DOM - 1, 1)
    base = jax.random.uniform(jax.random.fold_in(key, 3), (FACES, ELEMS), jnp.float32, 0.5, 1.5)
    return base * ramp[None, :]


def draw_face_link(key, part):
    kind = jax.random.randint(jax.random.fold_in(key, 11), (FACES, ELEMS), 0, 20)
    local_pick = jax.random.randint(jax.random.fold_in(key, 12), (FACES, ELEMS), 0, 4 * E_DEV)
    remote_pick = 4 * E_DEV + jax.random.randint(jax.random.fold_in(key, 13), (FACES, ELEMS), 0, PEERS * SLOTS)
    boundary = jnp.full((FACES, ELEMS), 4 * E_DEV + PEERS * SLOTS, jnp.int32)
    return jnp.where(kind < 13, local_pick, jnp.where(kind < 19, remote_pick, boundary)).astype(jnp.int32)


def draw_send_index(key, part):
    kind = jax.random.randint(jax.random.fold_in(key, 21), (N_DOM, PEERS, SLOTS), 0, 10)
    picked = jax.random.randint(jax.random.fold_in(key, 22), (N_DOM, PEERS, SLOTS), 0, 4 * E_DEV)
    return jnp.where(kind < 8, picked, 4 * E_DEV).astype(jnp.int32)


def draw_live_count(key, part):
    counts = jax.random.randint(jax.random.fold_in(key, 31), (N_DOM,), E_DEV // 2, E_DEV + 1)
    chosen = jax.random.randint(jax.random.fold_in(key, 32), (), 0, N_DOM)
    return jnp.where(jnp.arange(N_DOM) == chosen, E_DEV, counts).astype(jnp.int32)


def draw_mass_matrix(key, part):
    raw = jax.random.uniform(jax.random.fold_in(key, 41), (NODES, NODES), jnp.float32, -0.02, 0.02)
    symmetric = raw + raw.T
    eye_part = jnp.eye(NODES, dtype=jnp.float32)
    return symmetric * (1.0 - eye_part) + eye_part


def plant(values, rng, smallest, high):
    spot = [jax.random.randint(jax.random.fold_in(rng, axis), (), 0, length) for axis, length in enumerate(values.shape)]
    widest = values.shape.index(max(values.shape))
    beside = spot[:widest] + [(spot[widest] + 1) % values.shape[widest]] + spot[widest + 1:]
    return values.at[tuple(spot)].set(smallest).at[tuple(beside)].set(high)


def level_of(own_key, shape, cuts, least, largest):
    loudness = 1.0
    for dim, parts in cuts:
        draws = jax.random.uniform(jax.random.fold_in(jax.random.fold_in(own_key, 6), dim), (parts,), jnp.float32, least / len(cuts), largest / len(cuts))
        loudness = loudness * jnp.repeat(jnp.exp(draws), shape[dim] // parts).reshape((-1,) + (1,) * (len(shape) - 1 - dim))
    return loudness


def scatter_about(own_key, extent, spread, most, cuts=(), kind=jnp.bfloat16):
    factor_of = level_of(own_key, extent, cuts, -0.22, 0.18) if cuts else 1.0
    values = jax.random.normal(own_key, extent, jnp.float32) * spread * factor_of
    return jnp.minimum(jnp.maximum(values, -most), most).astype(kind)


def setup_inputs(seed: int = 0) -> dict:
    key_of = jax.random.split(jax.random.key(seed), 11)
    return {
        "source": scatter_about(key_of[0], (GASES, COMPS, NODES, ELEMS), 1.0, 6.0, ((3, 512),), jnp.float32),
        "absorption": jnp.clip(jnp.exp(math.log(4.0) - 2.0794415 * jax.random.uniform(key_of[1], (GASES, ELEMS), jnp.float32) ** level_of(key_of[1], (GASES, ELEMS), ((1, 512),), -0.2, 0.2)), 0.5, 4.0),
        "geometry": jnp.clip(0.2 + 0.400000021 * jax.random.uniform(key_of[2], (3, ELEMS), jnp.float32) ** level_of(key_of[2], (3, ELEMS), ((1, 512),), -0.2, 0.2), 0.2, 0.6),
        "penalty": draw_penalty(jax.random.fold_in(key_of[10], 71), 0),
        "face_link": draw_face_link(jax.random.fold_in(key_of[10], 71), 0),
        "face_orient": plant(jax.random.randint(key_of[5], (FACES, ELEMS), 0, 6), jax.random.fold_in(key_of[5], 1), 0, 5).astype(jnp.int32),
        "send_index": draw_send_index(jax.random.fold_in(key_of[10], 71), 0),
        "live_count": draw_live_count(jax.random.fold_in(key_of[10], 71), 0),
        "mass_matrix": draw_mass_matrix(jax.random.fold_in(key_of[10], 71), 0),
        "stiffness": scatter_about(key_of[9], (3, NODES, NODES), NODES ** -0.5, 1.25, (), jnp.float32),
    }


def node_tables():
    triangle = [(a, b, 3 - a - b) for a in range(4) for b in range(4 - a)]
    tetra_nodes = [(i, j, k, 3 - i - j - k) for i in range(4) for j in range(4 - i) for k in range(4 - i - j)]
    face_index = np.zeros((10, 4), np.int32)
    for t in range(10):
        for f in range(4):
            coords = list(triangle[t])
            coords.insert(f, 0)
            face_index[t, f] = tetra_nodes.index(tuple(coords))
    orders = ((0, 1, 2), (1, 2, 0), (2, 0, 1), (0, 2, 1), (2, 1, 0), (1, 0, 2))
    turned = np.zeros((6, 10), np.int32)
    for o in range(6):
        for t in range(10):
            turned[o, t] = triangle.index(tuple((triangle[t][q] for q in orders[o])))
    lifting = np.zeros((20, 40), np.float32)
    for t in range(10):
        for f in range(4):
            lifting[face_index[t, f], t * 4 + f] = 1.0
    return (face_index, turned, lifting)

def face_traces(field):
    face_index, turned, lifting = node_tables()
    count = field.shape[2]
    picked = field[:, face_index.reshape(-1), :]
    return picked.reshape(field.shape[0], 10, 4 * count)

def pack(traces, send_rows):
    blank = jnp.zeros((traces.shape[0], 10, 1), jnp.float32)
    trace_table = jnp.concatenate([traces, blank], axis=2)
    picked = jnp.take(trace_table, send_rows.reshape(-1), axis=2)
    return picked.reshape(traces.shape[0], 10, send_rows.shape[0], send_rows.shape[1])

def coefficient(absorption):
    scale = jnp.array([1.0, 3.0, 3.0, 3.0], jnp.float32)
    return (absorption[:, None, :] * scale[None, :, None]).reshape(-1, absorption.shape[1])

def local_apply(field, received, absorption, geometry, penalty, link, orient, live_mask, mass_matrix, stiffness):
    face_index, turned, lifting = node_tables()
    chans = field.shape[0]
    count = field.shape[2]
    traces = face_traces(field)
    blank = jnp.zeros((chans, 10, 1), jnp.float32)
    trace_table = jnp.concatenate([traces, received, blank], axis=2)
    width = trace_table.shape[2]
    table_flat = trace_table.reshape(chans, 10 * width)
    turned_rows = jnp.take(jnp.asarray(turned, jnp.int32), orient.astype(jnp.int32), axis=0)
    turned_rows = jnp.moveaxis(turned_rows, -1, 0)
    column = (turned_rows * width + link.astype(jnp.int32)[None]).astype(jnp.int32)
    chosen = jnp.take(table_flat, column.reshape(-1), axis=1).reshape(chans, 10, 4, count)
    own_trace = traces.reshape(chans, 10, 4, count)
    jump_term = (penalty[None, None] * (own_trace - chosen)).reshape(chans, 40, count)
    lift_matrix = jnp.asarray(lifting, jnp.float32)
    contrib = jnp.einsum('nk,ckx->cnx', lift_matrix, jump_term, precision=lax.Precision.HIGHEST)
    massed = jnp.einsum('mn,cnx->cmx', mass_matrix, field, precision=lax.Precision.HIGHEST)
    pieces = field.reshape(4, 4, 20, count)
    flux_terms = jnp.einsum('dmn,gdnx->gdmx', stiffness, pieces[:, 1:], precision=lax.Precision.HIGHEST)
    toward = jnp.sum(flux_terms * geometry[None, :, None, :], axis=1)
    backward = jnp.einsum('dnm,gnx->gdmx', stiffness, pieces[:, 0], precision=lax.Precision.HIGHEST)
    backward = backward * geometry[None, :, None, :]
    transport = jnp.concatenate([toward[:, None], -backward], axis=1).reshape(chans, 20, count)
    total = coefficient(absorption)[:, None, :] * massed + transport + contrib
    return live_mask * total

def precondition(res, absorption, penalty, mass_inverse):
    denom = coefficient(absorption) + 0.5 * jnp.sum(penalty, axis=0)[None, :]
    solved = jnp.einsum('mn,cnx->cmx', mass_inverse, res, precision=lax.Precision.HIGHEST)
    return solved / denom[:, None, :]

def inverse_mass(mass_matrix):
    factor = jnp.linalg.cholesky(mass_matrix)
    identity = jnp.eye(mass_matrix.shape[0], dtype=mass_matrix.dtype)
    lower_solved = lax.linalg.triangular_solve(factor, identity, left_side=True, lower=True)
    return lax.linalg.triangular_solve(factor, lower_solved, left_side=True, lower=True, transpose_a=True)

def peer_offset(p, reach):
    return p + 1 if p < reach else -(p - reach + 1)

def shift_devices(stack, offset):
    shape = stack.shape
    if offset > 0:
        zeros_part = jnp.zeros((offset,) + shape[1:], jnp.float32)
        return jnp.concatenate([zeros_part, stack[:-offset]], axis=0)
    zeros_part = jnp.zeros((-offset,) + shape[1:], jnp.float32)
    return jnp.concatenate([stack[-offset:], zeros_part], axis=0)

def reference(source, absorption, geometry, penalty, face_link, face_orient, send_index, live_count, mass_matrix, stiffness):

    def split(array):
        array = array.reshape(array.shape[:-1] + (N_DOM, E_DEV))
        return jnp.moveaxis(array, -2, 0)
    chans = GASES * COMPS
    source_dev = split(source.reshape(chans, NODES, ELEMS))
    absorb_dev = split(absorption)
    geom_dev = split(geometry)
    penal_dev = split(penalty)
    link_dev = split(face_link)
    orient_dev = split(face_orient)
    live_mask = (jnp.arange(E_DEV)[None, :] < live_count[:, None]).astype(jnp.float32)
    mass_inverse = inverse_mass(mass_matrix)

    def apply_all(field):
        outgoing = lax.map(lambda a: pack(face_traces(a[0]), a[1]), (field, send_index))
        pieces = []
        for p in range(PEERS):
            pieces.append(shift_devices(outgoing[:, :, :, p], peer_offset(p, REACH)))
        received = jnp.stack(pieces, axis=3).reshape(N_DOM, chans, 10, PEERS * SLOTS)
        return lax.map(lambda a: local_apply(a[0], a[1], a[2], a[3], a[4], a[5], a[6], a[7], mass_matrix, stiffness), (field, received, absorb_dev, geom_dev, penal_dev, link_dev, orient_dev, live_mask))

    def precondition_all(res):
        return lax.map(lambda a: precondition(a[0], a[1], a[2], mass_inverse), (res, absorb_dev, penal_dev))
    estimate = jnp.where(live_mask > 0.5, 1.0 + 0.25 * jnp.sum(penal_dev, axis=1), 0.0)
    upper = jnp.max(estimate)
    lower = 0.1 * upper
    centre = (upper + lower) / 2.0
    half_width = (upper - lower) / 2.0
    sigma_one = centre / half_width
    ratio_now = 1.0 / sigma_one
    solution = jnp.zeros_like(source_dev)
    residual = live_mask[:, None, None, :] * source_dev
    direction = precondition_all(residual) / centre
    for step in range(ITERS):
        solution = solution + direction
        residual = residual - apply_all(direction)
        if step < ITERS - 1:
            ratio_new = 1.0 / (2.0 * sigma_one - ratio_now)
            direction = ratio_new * ratio_now * direction + 2.0 * ratio_new / half_width * precondition_all(residual)
            ratio_now = ratio_new

    def merge(array):
        return jnp.moveaxis(array, 0, -2).reshape(GASES, COMPS, NODES, ELEMS)
    return (merge(solution), merge(residual))
```

```python
import functools

import jax
import jax.numpy as jnp
import numpy as np
from jax import lax
from jax.experimental import pallas as pl
from jax.experimental.pallas import tpu as pltpu
from jax.sharding import PartitionSpec as P

MESH = pl.DeviceIdType.MESH
F32 = jnp.float32
BF16 = jnp.bfloat16
GASES = 4
COMPS = 4
NODES = 20
FACES = 4
TRI = 10
SLOTS = 32
PEERS = 8
LANES = 128
OFFSETS = tuple(q + 1 if q < 4 else -(q - 3) for q in range(PEERS))
LOCAL = FACES * LANES
REMOTE = PEERS * SLOTS
ROWS = 2 * TRI * 8
PART = ROWS // 4
FIELD = NODES * 8


def node_tables():
    triangle = [(a, b, 3 - a - b) for a in range(4) for b in range(4 - a)]
    tetra_nodes = [
        (i, j, k, 3 - i - j - k) for i in range(4) for j in range(4 - i) for k in range(4 - i - j)
    ]
    face_index = np.zeros((10, 4), np.int32)
    for t in range(10):
        for f in range(4):
            coords = list(triangle[t])
            coords.insert(f, 0)
            face_index[t, f] = tetra_nodes.index(tuple(coords))
    orders = ((0, 1, 2), (1, 2, 0), (2, 0, 1), (0, 2, 1), (2, 1, 0), (1, 0, 2))
    turned = np.zeros((6, 10), np.int32)
    for o in range(6):
        for t in range(10):
            turned[o, t] = triangle.index(tuple((triangle[t][q] for q in orders[o])))
    return face_index.tolist(), turned.tolist()


FACE_NODE, TURNED = node_tables()


def radices(count):
    digits = []
    while count > 1:
        digit = 8 if count % 8 == 0 else count
        digits.append(digit)
        count //= digit
    return digits


def iota(shape, axis):
    return lax.broadcasted_iota(jnp.int32, shape, axis)


def split(value):
    high = value.astype(BF16).astype(F32)
    return high, value - high


def dot(a, b):
    return jnp.dot(a, b, preferred_element_type=F32)


def invert(matrix):
    size = matrix.shape[0]
    row_id, col_id = iota((size, size), 0), iota((size, size), 1)
    for k in range(size):
        pivot = 1.0 / matrix[k : k + 1, k : k + 1]
        row = jnp.where(col_id[:1] == k, 1.0, matrix[k : k + 1, :]) * pivot
        col = jnp.where(row_id[:, :1] == k, 0.0, matrix[:, k : k + 1])
        rest = jnp.where(col_id == k, 0.0, matrix) - col * row
        matrix = jnp.where(row_id == k, row, rest)
    return matrix


def spread_rows():
    return (iota((FIELD, NODES), 0) // 8 == iota((FIELD, NODES), 1)).astype(F32).astype(BF16)


def spread_columns():
    shape = (3 * NODES, 3 * FIELD)
    return (iota(shape, 1) // 8 == iota(shape, 0)).astype(F32).astype(BF16)


def thrice(matrix):
    high, low = split(matrix)
    return jnp.concatenate([high, high, low], axis=1).astype(BF16)


def times(weights, field):
    high, low = split(field)
    return dot(weights, jnp.concatenate([high, low, high], axis=0).astype(BF16))


def pair_up(first, second):
    sub = iota(first.shape, 1)
    even = jnp.where(sub < 4, first, pltpu.roll(second, 4, 1))
    odd = jnp.where(sub < 4, pltpu.roll(first, 4, 1), second)
    return even, odd


def kernel(
    n,
    source,
    absorption,
    geometry,
    penalty,
    link,
    orient,
    send_index,
    live_count,
    mass,
    stiffness,
    solution_out,
    residual_out,
    source_v,
    absorption_v,
    geometry_v,
    penalty_v,
    link_v,
    orient_v,
    send_v,
    mass_v,
    stiffness_v,
    rhs,
    direction,
    applied,
    second,
    mass_weights,
    flux_weights,
    pick_send,
    pick_local,
    pick_remote,
    table,
    outgoing,
    incoming,
    best,
    best_in,
    sol_v,
    res_v,
    in_sem,
    out_sem,
    send_sem,
    recv_sem,
    best_send,
    best_recv,
):
    me = lax.axis_index("dom")
    peers = [lax.rem(me + o + n, n) for o in OFFSETS]
    digits = radices(n)
    groups = []
    weight = 1
    for digit in digits:
        mine = lax.rem(me // weight, digit)
        groups.append(
            [me + (lax.rem(mine + k, digit) - mine) * weight for k in range(1, digit)]
        )
        weight *= digit

    barrier = pltpu.get_barrier_semaphore()
    everyone = peers + [d for group in groups for d in group]
    for device in everyone:
        pl.semaphore_signal(barrier, inc=1, device_id=(device,), device_id_type=MESH)

    loads = []
    for i, (src, dst) in enumerate(
        (
            (mass, mass_v),
            (source, source_v),
            (absorption, absorption_v),
            (penalty, penalty_v),
            (send_index, send_v),
            (geometry, geometry_v),
            (link, link_v),
            (orient, orient_v),
            (stiffness, stiffness_v),
        )
    ):
        copy = pltpu.make_async_copy(src, dst, in_sem.at[i])
        copy.start()
        loads.append(copy)
    for copy in loads:
        copy.wait()

    rows = spread_rows()
    columns = spread_columns()
    inverse = thrice(invert(mass_v[...]))
    square = (FIELD, 3 * FIELD)
    lane_of, row_of = iota(square, 1), iota(square, 0)
    wide = dot(dot(rows, inverse).astype(BF16), columns)
    mass_weights[...] = jnp.where(lane_of % 8 == row_of % 8, wide, 0.0).astype(BF16)

    live = (iota((1, LANES), 1) < live_count[0]).astype(F32)
    pen = [penalty_v[f : f + 1, :] for f in range(FACES)]
    pen_sum = pen[0] + pen[1] + pen[2] + pen[3]
    best[0] = jnp.where(live > 0.5, 1.0 + 0.25 * pen_sum, 0.0)
    sub = iota((8, LANES), 0)
    scale = jnp.where(sub % 4 == 0, 1.0, 3.0)
    coef = jnp.concatenate(
        [
            jnp.where(
                sub < 4,
                absorption_v[2 * pair : 2 * pair + 1, :],
                absorption_v[2 * pair + 1 : 2 * pair + 2, :],
            )
            * scale
            for pair in range(2)
        ],
        axis=1,
    )
    pen_sum_two = jnp.concatenate([pen_sum, pen_sum], axis=1)
    live_two = jnp.concatenate([live, live], axis=1)
    inv_denom = 1.0 / (coef + 0.5 * pen_sum_two)
    ratio = coef * inv_denom

    for pair in range(2):
        first = source_v[pl.ds(160 * pair, 80), :].reshape(10, 8, LANES)
        other = source_v[pl.ds(160 * pair + 80, 80), :].reshape(10, 8, LANES)
        even, odd = pair_up(first, other)
        lanes = pl.ds(pair * LANES, LANES)
        for p in range(10):
            rhs[2 * p, :, lanes] = even[p] * live
            rhs[2 * p + 1, :, lanes] = odd[p] * live

    def precondition(value, target):
        solved = times(mass_weights[...], value.reshape(FIELD, 2 * LANES))
        target[...] = solved.reshape(NODES, 8, 2 * LANES) * inv_denom[None]

    def fill_table(field):
        high, low = split(field[...])
        for h, part in enumerate((high, low)):
            for pair in range(2):
                block = jnp.concatenate(
                    [
                        jnp.concatenate(
                            [
                                part[FACE_NODE[t][f], :, pair * LANES : (pair + 1) * LANES]
                                for f in range(FACES)
                            ],
                            axis=1,
                        )
                        for t in range(TRI)
                    ],
                    axis=0,
                )
                table[pl.ds(h * ROWS + pair * 80, 80), :] = block.astype(BF16)

    group_of = iota((PART, LANES), 1) // SLOTS

    def pack(trade):
        both = dot(table[...], pick_send[...])
        packed = both[:ROWS] + both[ROWS:]
        for half in range(2):
            parts = [
                packed[j * PART : (j + 1) * PART, half * LANES : (half + 1) * LANES]
                for j in range(4)
            ]
            for q in range(4):
                message = None
                for j in range(4):
                    shift = (j - q) * SLOTS % LANES
                    part = pltpu.roll(parts[j], shift, 1) if shift else parts[j]
                    message = part if message is None else jnp.where(group_of == j, part, message)
                outgoing[trade, half * 4 + q] = message

    def unpack(trade):
        blocks = []
        for j in range(4):
            halves = []
            for half in range(2):
                gathered = None
                for q in range(4):
                    shift = (q - j) * SLOTS % LANES
                    part = incoming[trade, half * 4 + q]
                    part = pltpu.roll(part, shift, 1) if shift else part
                    gathered = part if gathered is None else jnp.where(group_of == q, part, gathered)
                halves.append(gathered)
            blocks.append(jnp.concatenate(halves, axis=1))
        received = jnp.concatenate(blocks, axis=0)
        high, low = split(received)
        return jnp.concatenate([high, low], axis=0).astype(BF16)

    def trade_copies(trade):
        return [
            pltpu.make_async_remote_copy(
                src_ref=outgoing.at[trade, q],
                dst_ref=incoming.at[trade, q],
                send_sem=send_sem.at[trade, q],
                recv_sem=recv_sem.at[trade, q],
                device_id=(peers[q],),
                device_id_type=MESH,
            )
            for q in range(PEERS)
        ]

    slot_at = []
    total = 0
    for digit in digits:
        slot_at.append(total)
        total += digit - 1

    def best_copies(level):
        return [
            pltpu.make_async_remote_copy(
                src_ref=best.at[level],
                dst_ref=best_in.at[slot_at[level] + k],
                send_sem=best_send.at[slot_at[level] + k],
                recv_sem=best_recv.at[slot_at[level] + k],
                device_id=(device,),
                device_id_type=MESH,
            )
            for k, device in enumerate(groups[level])
        ]

    def best_merge(level, copies):
        value = best[level]
        for k, copy in enumerate(copies):
            copy.wait_recv()
            value = jnp.maximum(value, best_in[slot_at[level] + k])
        best[level + 1] = value

    precondition(rhs[...], direction)

    sends = send_v[0]
    four = jnp.concatenate([sends, sends, sends, sends], axis=1)
    slot_q, slot_lane = iota((PEERS, LANES), 0), iota((PEERS, LANES), 1)
    for half in range(2):
        keep = slot_q == half * 4 + slot_lane // SLOTS
        chosen = jnp.sum(jnp.where(keep, four, 0), axis=0, keepdims=True)
        pick = iota((LOCAL, LANES), 0) == chosen
        pick_send[:, pl.ds(half * LANES, LANES)] = pick.astype(F32).astype(BF16)

    fill_table(direction)
    pack(0)

    pl.semaphore_wait(barrier, len(everyone))
    trades = [trade_copies(0), trade_copies(1)]
    for copy in trades[0]:
        copy.start()
    rounds = [best_copies(level) for level in range(len(digits))]
    for copy in rounds[0]:
        copy.start()

    for f in range(FACES):
        lanes = pl.ds(f * LANES, LANES)
        wanted = link_v[f : f + 1, :]
        pick_local[:, lanes] = (iota((LOCAL, LANES), 0) == wanted).astype(F32).astype(BF16)
        for q in range(PEERS):
            origin = me - OFFSETS[q]
            inside = jnp.logical_and(origin >= 0, origin < n).astype(F32)
            pick = (iota((SLOTS, LANES), 0) + (LOCAL + q * SLOTS) == wanted).astype(F32)
            pick_remote[pl.ds(q * SLOTS, SLOTS), lanes] = (pick * inside).astype(BF16)

    flux = jnp.zeros(square, F32)
    for d in range(3):
        ahead = thrice(stiffness_v[d])
        back = thrice(stiffness_v[d].T)
        from_flux = (row_of % 8) + (d + 1) == lane_of % 8
        from_flux = jnp.logical_and(from_flux, row_of % 4 == 0)
        to_flux = (lane_of % 8) + (d + 1) == row_of % 8
        to_flux = jnp.logical_and(to_flux, lane_of % 4 == 0)
        flux = jnp.where(from_flux, dot(dot(rows, ahead).astype(BF16), columns), flux)
        flux = jnp.where(to_flux, dot(dot(rows, back).astype(BF16), columns), flux)
    flux_weights[...] = flux.astype(BF16)

    geo = jnp.concatenate([geometry_v[d : d + 1, :] for d in range(3)], axis=0)
    geo_in = jnp.where(sub % 4 == 0, 1.0, 0.0)
    geo_out = geo_in
    for d in range(3):
        here = sub % 4 == d + 1
        geo_in = jnp.where(here, geo[d : d + 1], geo_in)
        geo_out = jnp.where(here, -geo[d : d + 1], geo_out)
    geo_in = jnp.concatenate([geo_in, geo_in], axis=1)
    geo_out = jnp.concatenate([geo_out, geo_out], axis=1)

    pen_node = []
    for node in range(NODES):
        value = None
        for t in range(TRI):
            for f in range(FACES):
                if FACE_NODE[t][f] == node:
                    value = pen[f] if value is None else value + pen[f]
        pen_node.append(jnp.concatenate([value, value], axis=1))
    pen_row = jnp.concatenate(pen, axis=1)
    orient_row = jnp.concatenate([orient_v[f : f + 1, :] for f in range(FACES)], axis=1)

    def apply_local(field):
        both = dot(table[...], pick_local[...])
        value = field[...]
        flux_term = times(flux_weights[...], (value * geo_in[None]).reshape(FIELD, 2 * LANES))
        return both[:ROWS] + both[ROWS:], flux_term.reshape(NODES, 8, 2 * LANES)

    def apply_remote(field, solved, local, received, target):
        near, flux_term = local
        both = dot(received, pick_remote[...])
        across = near + both[:ROWS] + both[ROWS:]
        total = [None] * NODES
        for t in range(TRI):
            sides = []
            for pair in range(2):
                def rows_of(node):
                    start = pair * 80 + node * 8
                    return across[start : start + 8]

                side = rows_of(TURNED[0][t])
                for o in range(1, 6):
                    if TURNED[o][t] != TURNED[0][t]:
                        side = jnp.where(orient_row == o, rows_of(TURNED[o][t]), side)
                sides.append(side * pen_row)
            for f in range(FACES):
                lanes = slice(f * LANES, (f + 1) * LANES)
                jump = jnp.concatenate([side[:, lanes] for side in sides], axis=1)
                node = FACE_NODE[t][f]
                total[node] = jump if total[node] is None else total[node] + jump
        for node in range(NODES):
            value = ratio * solved[node] + geo_out * flux_term[node]
            value = value + pen_node[node] * field[node] - total[node]
            target[node] = live_two * value

    local = apply_local(direction)
    best_merge(0, rounds[0])
    if len(digits) > 1:
        for copy in rounds[1]:
            copy.start()
    for copy in trades[0]:
        copy.wait_recv()
    apply_remote(direction, rhs, local, unpack(0), applied)

    precondition(applied[...], second)
    fill_table(second)
    pack(1)
    for copy in trades[1]:
        copy.start()
    if len(digits) > 1:
        best_merge(1, rounds[1])
    if len(digits) > 2:
        for copy in rounds[2]:
            copy.start()
    local = apply_local(second)
    for copy in trades[1]:
        copy.wait_recv()
    twice = sol_v
    apply_remote(second, applied, local, unpack(1), twice)

    for level in range(2, len(digits)):
        best_merge(level, rounds[level])

    upper = jnp.max(best[len(digits)], axis=1, keepdims=True)
    lower = 0.1 * upper
    centre = (upper + lower) / 2.0
    half_width = (upper - lower) / 2.0
    sigma_one = centre / half_width
    ratio_now = 1.0 / sigma_one
    ratio_new = 1.0 / (2.0 * sigma_one - ratio_now)
    inv_centre = 1.0 / centre
    step = 2.0 * ratio_new / half_width
    first_weight = inv_centre + ratio_new * ratio_now * inv_centre + step
    second_weight = -step * inv_centre
    sol = first_weight * direction[...] + second_weight * second[...]
    res = rhs[...] - first_weight * applied[...] - second_weight * twice[...]
    for value, target in ((sol, source_v), (res, res_v)):
        for pair in range(2):
            lanes = slice(pair * LANES, (pair + 1) * LANES)
            for p in range(10):
                even, odd = value[2 * p, :, lanes], value[2 * p + 1, :, lanes]
                low, high = pair_up(even[None], odd[None])
                target[pl.ds(160 * pair + 8 * p, 8), :] = low[0]
                target[pl.ds(160 * pair + 80 + 8 * p, 8), :] = high[0]

    stores = [
        pltpu.make_async_copy(source_v, solution_out, out_sem.at[0]),
        pltpu.make_async_copy(res_v, residual_out, out_sem.at[1]),
    ]
    for copy in stores:
        copy.start()
    for copies in trades + rounds:
        for copy in copies:
            copy.wait_send()
    for copy in stores:
        copy.wait()


def solution(mesh):
    n = mesh.shape["dom"]
    digits = radices(n)
    links = sum(digits) - len(digits)

    def body(
        source, absorption, geometry, penalty, link, orient, send_index, live_count, mass, stiffness
    ):
        flat = source.transpose(0, 2, 1, 3).reshape(GASES * NODES * COMPS, LANES)
        anywhere = pl.BlockSpec(memory_space=pl.ANY)
        vmem = pltpu.VMEM
        outs = pl.pallas_call(
            functools.partial(kernel, n),
            out_shape=[jax.ShapeDtypeStruct(flat.shape, F32)] * 2,
            in_specs=[anywhere] * 7
            + [pl.BlockSpec(memory_space=pltpu.SMEM)]
            + [anywhere] * 2,
            out_specs=[anywhere] * 2,
            scratch_shapes=[
                vmem((320, LANES), F32),
                vmem((4, LANES), F32),
                vmem((3, LANES), F32),
                vmem((4, LANES), F32),
                vmem((4, LANES), jnp.int32),
                vmem((4, LANES), jnp.int32),
                vmem((1, PEERS, SLOTS), jnp.int32),
                vmem((NODES, NODES), F32),
                vmem((3, NODES, NODES), F32),
                vmem((NODES, 8, 2 * LANES), F32),
                vmem((NODES, 8, 2 * LANES), F32),
                vmem((NODES, 8, 2 * LANES), F32),
                vmem((NODES, 8, 2 * LANES), F32),
                vmem((FIELD, 3 * FIELD), BF16),
                vmem((FIELD, 3 * FIELD), BF16),
                vmem((LOCAL, REMOTE), BF16),
                vmem((LOCAL, LOCAL), BF16),
                vmem((REMOTE, LOCAL), BF16),
                vmem((2 * ROWS, LOCAL), BF16),
                vmem((2, PEERS, PART, LANES), F32),
                vmem((2, PEERS, PART, LANES), F32),
                vmem((len(digits) + 1, 1, LANES), F32),
                vmem((links, 1, LANES), F32),
                vmem((NODES, 8, 2 * LANES), F32),
                vmem((320, LANES), F32),
                pltpu.SemaphoreType.DMA((9,)),
                pltpu.SemaphoreType.DMA((2,)),
                pltpu.SemaphoreType.DMA((2, PEERS)),
                pltpu.SemaphoreType.DMA((2, PEERS)),
                pltpu.SemaphoreType.DMA((links,)),
                pltpu.SemaphoreType.DMA((links,)),
            ],
            compiler_params=pltpu.CompilerParams(
                collective_id=0, has_side_effects=True, vmem_limit_bytes=32 * 2**20
            ),
            cost_estimate=pl.CostEstimate(
                flops=2_000_000_000, bytes_accessed=1_000_000, transcendentals=0
            ),
        )(flat, absorption, geometry, penalty, link, orient, send_index, live_count, mass, stiffness)
        return tuple(
            out.reshape(GASES, NODES, COMPS, LANES).transpose(0, 2, 1, 3) for out in outs
        )

    in_specs = (
        P(None, None, None, "dom"),
        P(None, "dom"),
        P(None, "dom"),
        P(None, "dom"),
        P(None, "dom"),
        P(None, "dom"),
        P("dom", None, None),
        P("dom"),
        P(),
        P(),
    )
    out_specs = (P(None, None, None, "dom"), P(None, None, None, "dom"))
    return jax.shard_map(body, mesh=mesh, in_specs=in_specs, out_specs=out_specs, check_vma=False)
```

```python
import functools

import jax
import jax.numpy as jnp
import numpy as np
from jax import lax
from jax.experimental import pallas as pl
from jax.experimental.pallas import tpu as pltpu
from jax.sharding import PartitionSpec as P

MESH = pl.DeviceIdType.MESH
F32 = jnp.float32
BF16 = jnp.bfloat16
GASES = 4
COMPS = 4
NODES = 20
FACES = 4
TRI = 10
SLOTS = 32
PEERS = 8
LANES = 128
OFFSETS = tuple(q + 1 if q < 4 else -(q - 3) for q in range(PEERS))
LOCAL = FACES * LANES
REMOTE = PEERS * SLOTS
ROWS = 2 * TRI * 8
PART = ROWS // 4
FIELD = NODES * 8


def node_tables():
    triangle = [(a, b, 3 - a - b) for a in range(4) for b in range(4 - a)]
    tetra_nodes = [
        (i, j, k, 3 - i - j - k) for i in range(4) for j in range(4 - i) for k in range(4 - i - j)
    ]
    face_index = np.zeros((10, 4), np.int32)
    for t in range(10):
        for f in range(4):
            coords = list(triangle[t])
            coords.insert(f, 0)
            face_index[t, f] = tetra_nodes.index(tuple(coords))
    orders = ((0, 1, 2), (1, 2, 0), (2, 0, 1), (0, 2, 1), (2, 1, 0), (1, 0, 2))
    turned = np.zeros((6, 10), np.int32)
    for o in range(6):
        for t in range(10):
            turned[o, t] = triangle.index(tuple((triangle[t][q] for q in orders[o])))
    return face_index.tolist(), turned.tolist()


FACE_NODE, TURNED = node_tables()


ORDER = (3, 7, 2, 6, 1, 5, 0, 4)
CUBE = 4


def torus(count):
    chips = count // 2
    z = 16 if chips >= 256 else min(chips, 4)
    y = min(4, chips // z)
    return chips // (z * y), y, z


def iota(shape, axis):
    return lax.broadcasted_iota(jnp.int32, shape, axis)


def split(value):
    high = value.astype(BF16).astype(F32)
    return high, value - high


def dot(a, b):
    return jnp.dot(a, b, preferred_element_type=F32)


def invert(matrix):
    size = matrix.shape[0]
    row_id, col_id = iota((size, size), 0), iota((size, size), 1)
    for k in range(size):
        pivot = 1.0 / matrix[k : k + 1, k : k + 1]
        row = jnp.where(col_id[:1] == k, 1.0, matrix[k : k + 1, :]) * pivot
        col = jnp.where(row_id[:, :1] == k, 0.0, matrix[:, k : k + 1])
        rest = jnp.where(col_id == k, 0.0, matrix) - col * row
        matrix = jnp.where(row_id == k, row, rest)
    return matrix


def spread_rows():
    return (iota((FIELD, NODES), 0) // 8 == iota((FIELD, NODES), 1)).astype(F32).astype(BF16)


def spread_columns():
    shape = (3 * NODES, 3 * FIELD)
    return (iota(shape, 1) // 8 == iota(shape, 0)).astype(F32).astype(BF16)


def thrice(matrix):
    high, low = split(matrix)
    return jnp.concatenate([high, high, low], axis=1).astype(BF16)


def times(weights, field):
    high, low = split(field)
    return dot(weights, jnp.concatenate([high, low, high], axis=0).astype(BF16))


def pair_up(first, second):
    sub = iota(first.shape, 1)
    even = jnp.where(sub < 4, first, pltpu.roll(second, 4, 1))
    odd = jnp.where(sub < 4, pltpu.roll(first, 4, 1), second)
    return even, odd


def kernel(
    n,
    source,
    absorption,
    geometry,
    penalty,
    link,
    orient,
    send_index,
    live_count,
    mass,
    stiffness,
    solution_out,
    residual_out,
    source_v,
    absorption_v,
    geometry_v,
    penalty_v,
    link_v,
    orient_v,
    send_v,
    live_v,
    mass_v,
    stiffness_v,
    rhs,
    direction,
    applied,
    second,
    twice,
    mass_weights,
    flux_weights,
    pick_send,
    pick_local,
    pick_remote,
    table,
    outgoing,
    incoming,
    own_best,
    column_in,
    along_in,
    level,
    top,
    in_sem,
    send_sem,
    recv_sem,
    up_send,
    up_recv,
    along_send,
    along_recv,
    down_send,
    down_recv,
):
    me = lax.axis_index("dom")
    size_x, size_y, size_z = torus(n)
    core = lax.rem(me, 2)
    at_z = lax.rem(me // 2, size_z)
    at_y = lax.rem(me // (2 * size_z), size_y)
    at_x = me // (2 * size_z * size_y)

    def device(x, y, z, c):
        return ((x * size_y + y) * size_z + z) * 2 + c

    peers = [lax.rem(me + OFFSETS[q] + n, n) for q in ORDER]
    along_x = [device(lax.rem(at_x + k, size_x), at_y, at_z, core) for k in range(1, size_x)]
    along_y = [device(at_x, lax.rem(at_y + k, size_y), at_z, core) for k in range(1, size_y)]
    is_head = at_z == 0
    is_relay = jnp.logical_and(at_z > 0, lax.rem(at_z, CUBE) == 0)
    others = [(z, c) for z in range(1, size_z) for c in range(2)]

    barrier = pltpu.get_barrier_semaphore()

    def greet(target):
        pl.semaphore_signal(barrier, inc=1, device_id=(target,), device_id_type=MESH)

    for target in peers:
        greet(target)

    @pl.when(is_head)
    def _():
        greet(device(at_x, at_y, 0, 1 - core))
        for target in along_x + along_y:
            greet(target)
        for z, c in others:
            greet(device(at_x, at_y, z, c))

    loads = []
    for i, (src, dst) in enumerate(
        (
            (penalty, penalty_v),
            (live_count, live_v),
            (mass, mass_v),
            (send_index, send_v),
            (source, source_v),
            (absorption, absorption_v),
            (geometry, geometry_v),
            (link, link_v),
            (orient, orient_v),
            (stiffness, stiffness_v),
        )
    ):
        copy = pltpu.make_async_copy(src, dst, in_sem.at[i])
        copy.start()
        loads.append(copy)

    for copy in loads[:2]:
        copy.wait()
    live = (iota((1, LANES), 1) < live_v[0]).astype(F32)
    pen = [penalty_v[f : f + 1, :] for f in range(FACES)]
    pen_sum = pen[0] + pen[1] + pen[2] + pen[3]
    best = jnp.where(live > 0.5, 1.0 + 0.25 * pen_sum, 0.0)
    own_best[...] = best

    def remote(src, dst, send, recv, target):
        return pltpu.make_async_remote_copy(
            src_ref=src,
            dst_ref=dst,
            send_sem=send,
            recv_sem=recv,
            device_id=(target,),
            device_id_type=MESH,
        )

    mine = at_z * 2 + core
    up = [
        remote(
            own_best,
            column_in.at[mine],
            up_send.at[i],
            up_recv.at[mine],
            device(at_x, at_y, 0, c),
        )
        for i, c in enumerate((1 - core, core))
    ]

    @pl.when(is_head)
    def _():
        pl.semaphore_wait(barrier, PEERS + 1 + len(along_x) + len(along_y))
        up[0].start()

    @pl.when(jnp.logical_not(is_head))
    def _():
        pl.semaphore_wait(barrier, PEERS + 2)
        up[0].start()
        up[1].start()

    for copy in loads[2:]:
        copy.wait()

    rows = spread_rows()
    columns = spread_columns()
    inverse = thrice(invert(mass_v[...]))
    square = (FIELD, 3 * FIELD)
    lane_of, row_of = iota(square, 1), iota(square, 0)
    wide = dot(dot(rows, inverse).astype(BF16), columns)
    mass_weights[...] = jnp.where(lane_of % 8 == row_of % 8, wide, 0.0).astype(BF16)

    sends = send_v[0]
    four = jnp.concatenate([sends, sends, sends, sends], axis=1)
    slot_q, slot_group = iota((PEERS, LANES), 0), iota((PEERS, LANES), 1) // SLOTS
    for half in range(2):
        wanted = jnp.zeros((PEERS, LANES), jnp.int32)
        for g in range(4):
            wanted = jnp.where(slot_group == g, ORDER[half * 4 + g], wanted)
        chosen = jnp.sum(jnp.where(slot_q == wanted, four, 0), axis=0, keepdims=True)
        pick = iota((LOCAL, LANES), 0) == chosen
        pick_send[half] = pick.astype(F32).astype(BF16)

    for f in range(FACES):
        lanes = pl.ds(f * LANES, LANES)
        wanted = link_v[f : f + 1, :]
        pick_local[:, lanes] = (iota((LOCAL, LANES), 0) == wanted).astype(F32).astype(BF16)
        for place, q in enumerate(ORDER):
            origin = me - OFFSETS[q]
            inside = jnp.logical_and(origin >= 0, origin < n).astype(F32)
            pick = (iota((SLOTS, LANES), 0) + (LOCAL + q * SLOTS) == wanted).astype(F32)
            pick_remote[pl.ds(place * SLOTS, SLOTS), lanes] = (pick * inside).astype(BF16)

    sub = iota((8, LANES), 0)
    scale = jnp.where(sub % 4 == 0, 1.0, 3.0)
    coef = jnp.concatenate(
        [
            jnp.where(
                sub < 4,
                absorption_v[2 * pair : 2 * pair + 1, :],
                absorption_v[2 * pair + 1 : 2 * pair + 2, :],
            )
            * scale
            for pair in range(2)
        ],
        axis=1,
    )
    pen_sum_two = jnp.concatenate([pen_sum, pen_sum], axis=1)
    live_two = jnp.concatenate([live, live], axis=1)
    inv_denom = 1.0 / (coef + 0.5 * pen_sum_two)
    ratio = coef * inv_denom

    for pair in range(2):
        first = source_v[pl.ds(160 * pair, 80), :].reshape(10, 8, LANES)
        other = source_v[pl.ds(160 * pair + 80, 80), :].reshape(10, 8, LANES)
        even, odd = pair_up(first, other)
        lanes = pl.ds(pair * LANES, LANES)
        for p in range(10):
            rhs[2 * p, :, lanes] = even[p] * live
            rhs[2 * p + 1, :, lanes] = odd[p] * live

    def precondition(value, target):
        solved = times(mass_weights[...], value.reshape(FIELD, 2 * LANES))
        target[...] = solved.reshape(NODES, 8, 2 * LANES) * inv_denom[None]

    def fill_table(field):
        high, low = split(field[...])
        for h, part in enumerate((high, low)):
            for pair in range(2):
                block = jnp.concatenate(
                    [
                        jnp.concatenate(
                            [
                                part[FACE_NODE[t][f], :, pair * LANES : (pair + 1) * LANES]
                                for f in range(FACES)
                            ],
                            axis=1,
                        )
                        for t in range(TRI)
                    ],
                    axis=0,
                )
                table[pl.ds(h * ROWS + pair * 80, 80), :] = block.astype(BF16)

    group_of = iota((PART, LANES), 1) // SLOTS

    def trade_copies(trade):
        return [
            remote(
                outgoing.at[trade, place],
                incoming.at[trade, place],
                send_sem.at[trade, place],
                recv_sem.at[trade, place],
                peers[place],
            )
            for place in range(PEERS)
        ]

    trades = [trade_copies(0), trade_copies(1)]

    def send_traces(trade):
        for half in range(2):
            both = dot(table[...], pick_send[half])
            packed = both[:ROWS] + both[ROWS:]
            parts = [packed[j * PART : (j + 1) * PART] for j in range(4)]
            for g in range(4):
                message = None
                for j in range(4):
                    shift = (j - g) * SLOTS % LANES
                    part = pltpu.roll(parts[j], shift, 1) if shift else parts[j]
                    message = part if message is None else jnp.where(group_of == j, part, message)
                outgoing[trade, half * 4 + g] = message
            for copy in trades[trade][half * 4 : half * 4 + 4]:
                copy.start()

    def receive_traces(trade):
        for copy in trades[trade]:
            copy.wait_recv()
        blocks = []
        for j in range(4):
            halves = []
            for half in range(2):
                gathered = None
                for g in range(4):
                    shift = (g - j) * SLOTS % LANES
                    part = incoming[trade, half * 4 + g]
                    part = pltpu.roll(part, shift, 1) if shift else part
                    gathered = part if gathered is None else jnp.where(group_of == g, part, gathered)
                halves.append(gathered)
            blocks.append(jnp.concatenate(halves, axis=1))
        received = jnp.concatenate(blocks, axis=0)
        high, low = split(received)
        return jnp.concatenate([high, low], axis=0).astype(BF16)

    precondition(rhs[...], direction)
    fill_table(direction)
    send_traces(0)

    flux = jnp.zeros(square, F32)
    for d in range(3):
        ahead = thrice(stiffness_v[d])
        back = thrice(stiffness_v[d].T)
        from_flux = (row_of % 8) + (d + 1) == lane_of % 8
        from_flux = jnp.logical_and(from_flux, row_of % 4 == 0)
        to_flux = (lane_of % 8) + (d + 1) == row_of % 8
        to_flux = jnp.logical_and(to_flux, lane_of % 4 == 0)
        flux = jnp.where(from_flux, dot(dot(rows, ahead).astype(BF16), columns), flux)
        flux = jnp.where(to_flux, dot(dot(rows, back).astype(BF16), columns), flux)
    flux_weights[...] = flux.astype(BF16)

    geo_in = jnp.where(sub % 4 == 0, 1.0, 0.0)
    geo_out = geo_in
    for d in range(3):
        here = sub % 4 == d + 1
        geo_in = jnp.where(here, geometry_v[d : d + 1, :], geo_in)
        geo_out = jnp.where(here, -geometry_v[d : d + 1, :], geo_out)
    geo_in = jnp.concatenate([geo_in, geo_in], axis=1)
    geo_out = jnp.concatenate([geo_out, geo_out], axis=1)

    pen_node = []
    for node in range(NODES):
        value = None
        for t in range(TRI):
            for f in range(FACES):
                if FACE_NODE[t][f] == node:
                    value = pen[f] if value is None else value + pen[f]
        pen_node.append(jnp.concatenate([value, value], axis=1))
    pen_row = jnp.concatenate(pen, axis=1)
    orient_row = jnp.concatenate([orient_v[f : f + 1, :] for f in range(FACES)], axis=1)

    def apply_local(field):
        both = dot(table[...], pick_local[...])
        value = field[...]
        flux_term = times(flux_weights[...], (value * geo_in[None]).reshape(FIELD, 2 * LANES))
        return both[:ROWS] + both[ROWS:], flux_term.reshape(NODES, 8, 2 * LANES)

    def apply_remote(field, solved, local, received, target):
        near, flux_term = local
        both = dot(received, pick_remote[...])
        across = near + both[:ROWS] + both[ROWS:]
        total = [None] * NODES
        for t in range(TRI):
            sides = []
            for pair in range(2):
                def rows_of(node):
                    start = pair * 80 + node * 8
                    return across[start : start + 8]

                side = rows_of(TURNED[0][t])
                for o in range(1, 6):
                    if TURNED[o][t] != TURNED[0][t]:
                        side = jnp.where(orient_row == o, rows_of(TURNED[o][t]), side)
                sides.append(side * pen_row)
            for f in range(FACES):
                lanes = slice(f * LANES, (f + 1) * LANES)
                jump = jnp.concatenate([side[:, lanes] for side in sides], axis=1)
                node = FACE_NODE[t][f]
                total[node] = jump if total[node] is None else total[node] + jump
        for node in range(NODES):
            value = ratio * solved[node] + geo_out * flux_term[node]
            value = value + pen_node[node] * field[node] - total[node]
            target[node] = live_two * value

    local = apply_local(direction)
    apply_remote(direction, rhs, local, receive_traces(0), applied)
    precondition(applied[...], second)
    fill_table(second)
    send_traces(1)
    local = apply_local(second)

    def agree(value, first_slot, targets, slot):
        level[slot] = value
        copies = [
            remote(
                level.at[slot],
                along_in.at[first_slot + k],
                along_send.at[first_slot + k],
                along_recv.at[first_slot + k],
                target,
            )
            for k, target in enumerate(targets)
        ]
        for copy in copies:
            copy.start()
        for k, copy in enumerate(copies):
            copy.wait_recv()
            value = jnp.maximum(value, along_in[first_slot + k])
        return value, copies

    down_to = [z for z in (1, 8, 12, 4, 2, 3) if z < size_z]
    down = [
        remote(top, top, down_send.at[i], down_recv.at[0], device(at_x, at_y, z, core))
        for i, z in enumerate(down_to)
    ]
    relays = [
        remote(top, top, down_send.at[i], down_recv.at[0], device(at_x, at_y, at_z + i + 1, core))
        for i in range(CUBE - 1)
    ]

    def column_slot(slot):
        return remote(own_best, column_in.at[slot], up_send.at[0], up_recv.at[slot], peers[0])

    @pl.when(is_head)
    def _():
        value = own_best[...]
        for slot in [1 - core] + [2 * z + c for z, c in others]:
            column_slot(slot).wait_recv()
            value = jnp.maximum(value, column_in[slot])
        value, first = agree(value, 0, along_x, 0)
        value, then = agree(value, len(along_x), along_y, 1)
        top[...] = value
        for copy in down:
            copy.start()
        for copy in first + then:
            copy.wait_send()
        up[0].wait_send()

    apply_remote(second, applied, local, receive_traces(1), twice)

    @pl.when(jnp.logical_not(is_head))
    def _():
        down[0].wait_recv()
        up[0].wait_send()
        up[1].wait_send()

    @pl.when(is_relay)
    def _():
        for copy in relays:
            copy.start()

    upper = jnp.max(top[...], axis=1, keepdims=True)
    lower = 0.1 * upper
    centre = (upper + lower) / 2.0
    half_width = (upper - lower) / 2.0
    sigma_one = centre / half_width
    ratio_now = 1.0 / sigma_one
    ratio_new = 1.0 / (2.0 * sigma_one - ratio_now)
    inv_centre = 1.0 / centre
    step = 2.0 * ratio_new / half_width
    first_weight = inv_centre + ratio_new * ratio_now * inv_centre + step
    second_weight = -step * inv_centre
    sol = first_weight * direction[...] + second_weight * second[...]
    res = rhs[...] - first_weight * applied[...] - second_weight * twice[...]
    for value, target in ((sol, solution_out), (res, residual_out)):
        for pair in range(2):
            lanes = slice(pair * LANES, (pair + 1) * LANES)
            for p in range(10):
                even, odd = value[2 * p, :, lanes], value[2 * p + 1, :, lanes]
                low, high = pair_up(even[None], odd[None])
                target[pl.ds(160 * pair + 8 * p, 8), :] = low[0]
                target[pl.ds(160 * pair + 80 + 8 * p, 8), :] = high[0]

    for copies in trades:
        for copy in copies:
            copy.wait_send()

    @pl.when(is_head)
    def _():
        for copy in down:
            copy.wait_send()

    @pl.when(is_relay)
    def _():
        for copy in relays:
            copy.wait_send()


def solution(mesh):
    n = mesh.shape["dom"]
    size_x, size_y, size_z = torus(n)
    along = max(size_x + size_y - 2, 1)

    def body(
        source, absorption, geometry, penalty, link, orient, send_index, live_count, mass, stiffness
    ):
        flat = source.transpose(0, 2, 1, 3).reshape(GASES * NODES * COMPS, LANES)
        operands = (
            flat,
            absorption,
            geometry,
            penalty,
            link,
            orient,
            send_index,
            live_count,
            mass,
            stiffness,
        )
        vmem = pltpu.VMEM
        field = vmem((NODES, 8, 2 * LANES), F32)
        dma = pltpu.SemaphoreType.DMA
        outs = pl.pallas_call(
            functools.partial(kernel, n),
            out_shape=[jax.ShapeDtypeStruct(flat.shape, F32)] * 2,
            in_specs=[pl.BlockSpec(memory_space=pltpu.HBM)] * 10,
            out_specs=[pl.BlockSpec(memory_space=vmem)] * 2,
            scratch_shapes=[
                vmem((320, LANES), F32),
                vmem((4, LANES), F32),
                vmem((3, LANES), F32),
                vmem((4, LANES), F32),
                vmem((4, LANES), jnp.int32),
                vmem((4, LANES), jnp.int32),
                vmem((1, PEERS, SLOTS), jnp.int32),
                pltpu.SMEM((1,), jnp.int32),
                vmem((NODES, NODES), F32),
                vmem((3, NODES, NODES), F32),
                field,
                field,
                field,
                field,
                field,
                vmem((FIELD, 3 * FIELD), BF16),
                vmem((FIELD, 3 * FIELD), BF16),
                vmem((2, LOCAL, LANES), BF16),
                vmem((LOCAL, LOCAL), BF16),
                vmem((REMOTE, LOCAL), BF16),
                vmem((2 * ROWS, LOCAL), BF16),
                vmem((2, PEERS, PART, LANES), F32),
                vmem((2, PEERS, PART, LANES), F32),
                vmem((1, LANES), F32),
                vmem((2 * size_z, 1, LANES), F32),
                vmem((along, 1, LANES), F32),
                vmem((2, 1, LANES), F32),
                vmem((1, LANES), F32),
                dma((10,)),
                dma((2, PEERS)),
                dma((2, PEERS)),
                dma((2,)),
                dma((2 * size_z,)),
                dma((along,)),
                dma((along,)),
                dma((6,)),
                dma((1,)),
            ],
            compiler_params=pltpu.CompilerParams(
                collective_id=0, has_side_effects=True, vmem_limit_bytes=32 * 2**20
            ),
            cost_estimate=pl.CostEstimate(
                flops=2_000_000_000, bytes_accessed=1_000_000, transcendentals=0
            ),
        )(*[
                value if value is live_count else pltpu.with_memory_space_constraint(value, pltpu.HBM)
                for value in operands
            ]
        )
        return tuple(
            out.reshape(GASES, NODES, COMPS, LANES).transpose(0, 2, 1, 3) for out in outs
        )

    in_specs = (
        P(None, None, None, "dom"),
        P(None, "dom"),
        P(None, "dom"),
        P(None, "dom"),
        P(None, "dom"),
        P(None, "dom"),
        P("dom", None, None),
        P("dom"),
        P(),
        P(),
    )
    out_specs = (P(None, None, None, "dom"), P(None, None, None, "dom"))
    return jax.shard_map(body, mesh=mesh, in_specs=in_specs, out_specs=out_specs, check_vma=False)
```

```python
import functools

import jax
import jax.numpy as jnp
import numpy as np
from jax import lax
from jax.experimental import pallas as pl
from jax.experimental.pallas import tpu as pltpu
from jax.sharding import PartitionSpec as P

MESH = pl.DeviceIdType.MESH
F32 = jnp.float32
BF16 = jnp.bfloat16
GASES = 4
COMPS = 4
NODES = 20
FACES = 4
TRI = 10
SLOTS = 32
PEERS = 8
LANES = 128
OFFSETS = tuple(q + 1 if q < 4 else -(q - 3) for q in range(PEERS))
LOCAL = FACES * LANES
REMOTE = PEERS * SLOTS
ROWS = 2 * TRI * 8
PART = ROWS // 4
FIELD = NODES * 8


def node_tables():
    triangle = [(a, b, 3 - a - b) for a in range(4) for b in range(4 - a)]
    tetra_nodes = [
        (i, j, k, 3 - i - j - k) for i in range(4) for j in range(4 - i) for k in range(4 - i - j)
    ]
    face_index = np.zeros((10, 4), np.int32)
    for t in range(10):
        for f in range(4):
            coords = list(triangle[t])
            coords.insert(f, 0)
            face_index[t, f] = tetra_nodes.index(tuple(coords))
    orders = ((0, 1, 2), (1, 2, 0), (2, 0, 1), (0, 2, 1), (2, 1, 0), (1, 0, 2))
    turned = np.zeros((6, 10), np.int32)
    for o in range(6):
        for t in range(10):
            turned[o, t] = triangle.index(tuple((triangle[t][q] for q in orders[o])))
    return face_index.tolist(), turned.tolist()


FACE_NODE, TURNED = node_tables()


ORDER = (3, 7, 2, 6, 1, 5, 0, 4)
CUBE = 4
DOWN = {0: (12, 1, 2, 3), 4: (8, 5, 6, 7)}
EARLY = 4


def torus(count):
    chips = count // 2
    z = 16 if chips >= 256 else min(chips, 4)
    y = min(4, chips // z)
    return chips // (z * y), y, z


def iota(shape, axis):
    return lax.broadcasted_iota(jnp.int32, shape, axis)


def split(value):
    high = value.astype(BF16).astype(F32)
    return high, value - high


def dot(a, b):
    return jnp.dot(a, b, preferred_element_type=F32)


def invert(matrix):
    size = matrix.shape[0]
    lane, sub = iota((size, LANES), 1), iota((size, LANES), 0)
    planes = [jnp.broadcast_to(matrix[:, i : i + 1], (size, LANES)) for i in range(size)]
    state = jnp.stack(planes, axis=0)
    for k in range(size):
        pivot = 1.0 / state[k, k : k + 1]
        row = state[k] * pivot
        change = jnp.where(sub == k, 1.0 + pivot, row)
        row = jnp.where(sub == k, pivot, row)
        rest = state - state[:, k : k + 1, :] * change[None]
        state = jnp.concatenate(
            [part for part in (rest[:k], row[None], rest[k + 1 :]) if part.shape[0]], axis=0
        )
    inverse = state[0]
    for i in range(1, size):
        inverse = jnp.where(lane == i, state[i], inverse)
    return inverse[:, :size]


def spread_rows():
    return (iota((FIELD, NODES), 0) // 8 == iota((FIELD, NODES), 1)).astype(F32).astype(BF16)


def spread_columns():
    shape = (3 * NODES, 3 * FIELD)
    return (iota(shape, 1) // 8 == iota(shape, 0)).astype(F32).astype(BF16)


def thrice(matrix):
    high, low = split(matrix)
    return jnp.concatenate([high, high, low], axis=1).astype(BF16)


def times(weights, field):
    high, low = split(field)
    return dot(weights, jnp.concatenate([high, low, high], axis=0).astype(BF16))


def pair_up(first, second):
    sub = iota(first.shape, 1)
    even = jnp.where(sub < 4, first, pltpu.roll(second, 4, 1))
    odd = jnp.where(sub < 4, pltpu.roll(first, 4, 1), second)
    return even, odd


def kernel(
    n,
    source,
    absorption,
    geometry,
    penalty,
    link,
    orient,
    send_index,
    live_count,
    mass,
    stiffness,
    solution_out,
    residual_out,
    source_v,
    absorption_v,
    geometry_v,
    penalty_v,
    link_v,
    orient_v,
    send_v,
    live_v,
    mass_v,
    stiffness_v,
    rhs,
    direction,
    applied,
    second,
    twice,
    mass_weights,
    flux_weights,
    pick_send,
    pick_local,
    pick_remote,
    table,
    outgoing,
    incoming,
    own_best,
    column_in,
    along_in,
    level,
    top,
    in_sem,
    send_sem,
    recv_sem,
    up_send,
    up_recv,
    along_send,
    along_recv,
    down_send,
    down_recv,
):
    me = lax.axis_index("dom")
    size_x, size_y, size_z = torus(n)
    core = lax.rem(me, 2)
    at_z = lax.rem(me // 2, size_z)
    at_y = lax.rem(me // (2 * size_z), size_y)
    at_x = me // (2 * size_z * size_y)

    def device(x, y, z, c):
        return ((x * size_y + y) * size_z + z) * 2 + c

    def inside(index):
        return jnp.logical_and(index >= 0, index < n)

    targets = [me + OFFSETS[q] for q in ORDER]
    origins = [me - OFFSETS[q] for q in ORDER]
    along_x = [device(lax.rem(at_x + k, size_x), at_y, at_z, core) for k in range(1, size_x)]
    along_y = [device(at_x, lax.rem(at_y + k, size_y), at_z, core) for k in range(1, size_y)]
    planes = [z for z in DOWN if z < size_z]
    is_head = functools.reduce(jnp.logical_or, [at_z == z for z in planes])
    is_relay = jnp.logical_and(lax.rem(at_z, CUBE) == 0, jnp.logical_not(is_head))
    is_early = at_z < EARLY

    barrier = pltpu.get_barrier_semaphore()

    def greet(target):
        pl.semaphore_signal(barrier, inc=1, device_id=(target,), device_id_type=MESH)

    for target in targets:
        pl.when(inside(target))(functools.partial(greet, target))

    @pl.when(is_head)
    def _():
        greet(device(at_x, at_y, at_z, 1 - core))
        for target in along_x + along_y:
            greet(target)
        for k in range(1, size_z):
            for c in range(2):
                greet(device(at_x, at_y, lax.rem(at_z + k, size_z), c))

    loads = []
    for i, (src, dst) in enumerate(
        (
            (penalty, penalty_v),
            (live_count, live_v),
            (mass, mass_v),
            (send_index, send_v),
            (source, source_v),
            (absorption, absorption_v),
            (geometry, geometry_v),
            (link, link_v),
            (orient, orient_v),
            (stiffness, stiffness_v),
        )
    ):
        copy = pltpu.make_async_copy(src, dst, in_sem.at[i])
        copy.start()
        loads.append(copy)

    for copy in loads[:2]:
        copy.wait()
    live = (iota((1, LANES), 1) < live_v[0]).astype(F32)
    pen = [penalty_v[f : f + 1, :] for f in range(FACES)]
    pen_sum = pen[0] + pen[1] + pen[2] + pen[3]
    best = jnp.where(live > 0.5, 1.0 + 0.25 * pen_sum, 0.0)
    own_best[...] = best

    def remote(src, dst, send, recv, target):
        return pltpu.make_async_remote_copy(
            src_ref=src,
            dst_ref=dst,
            send_sem=send,
            recv_sem=recv,
            device_id=(target,),
            device_id_type=MESH,
        )

    mine = at_z * 2 + core
    up = [
        remote(
            own_best,
            column_in.at[mine],
            up_send.at[2 * i + c],
            up_recv.at[mine],
            device(at_x, at_y, z, c),
        )
        for i, z in enumerate(planes)
        for c in range(2)
    ]
    up_to = [jnp.logical_not(jnp.logical_and(at_z == z, core == c)) for z in planes for c in range(2)]
    partners = sum([inside(target).astype(jnp.int32) for target in targets])
    partners = partners + sum([wanted.astype(jnp.int32) for wanted in up_to])
    partners = partners + is_head.astype(jnp.int32) * (len(along_x) + len(along_y))

    def send_up():
        pl.semaphore_wait(barrier, partners)
        for wanted, copy in zip(up_to, up):
            pl.when(wanted)(copy.start)

    pl.when(jnp.logical_not(is_early))(send_up)

    for copy in loads[2:]:
        copy.wait()

    rows = spread_rows()
    columns = spread_columns()
    inverse = thrice(invert(mass_v[...]))
    square = (FIELD, 3 * FIELD)
    lane_of, row_of = iota(square, 1), iota(square, 0)
    wide = dot(dot(rows, inverse).astype(BF16), columns)
    mass_weights[...] = jnp.where(lane_of % 8 == row_of % 8, wide, 0.0).astype(BF16)

    sends = send_v[0]
    four = jnp.concatenate([sends, sends, sends, sends], axis=1)
    slot_q, slot_group = iota((PEERS, LANES), 0), iota((PEERS, LANES), 1) // SLOTS
    for half in range(2):
        wanted = jnp.zeros((PEERS, LANES), jnp.int32)
        for g in range(4):
            wanted = jnp.where(slot_group == g, ORDER[half * 4 + g], wanted)
        chosen = jnp.sum(jnp.where(slot_q == wanted, four, 0), axis=0, keepdims=True)
        pick = iota((LOCAL, LANES), 0) == chosen
        pick_send[half] = pick.astype(F32).astype(BF16)

    for f in range(FACES):
        lanes = pl.ds(f * LANES, LANES)
        wanted = link_v[f : f + 1, :]
        pick_local[:, lanes] = (iota((LOCAL, LANES), 0) == wanted).astype(F32).astype(BF16)
        for place, q in enumerate(ORDER):
            pick = iota((SLOTS, LANES), 0) + (LOCAL + q * SLOTS) == wanted
            pick_remote[pl.ds(place * SLOTS, SLOTS), lanes] = pick.astype(F32).astype(BF16)

    for place, origin in enumerate(origins):

        @pl.when(jnp.logical_not(inside(origin)))
        def _(place=place):
            for trade in range(2):
                incoming[trade, place] = jnp.zeros((PART, LANES), F32)

    sub = iota((8, LANES), 0)
    scale = jnp.where(sub % 4 == 0, 1.0, 3.0)
    coef = jnp.concatenate(
        [
            jnp.where(
                sub < 4,
                absorption_v[2 * pair : 2 * pair + 1, :],
                absorption_v[2 * pair + 1 : 2 * pair + 2, :],
            )
            * scale
            for pair in range(2)
        ],
        axis=1,
    )
    pen_sum_two = jnp.concatenate([pen_sum, pen_sum], axis=1)
    live_two = jnp.concatenate([live, live], axis=1)
    inv_denom = 1.0 / (coef + 0.5 * pen_sum_two)
    ratio = coef * inv_denom

    for pair in range(2):
        first = source_v[pl.ds(160 * pair, 80), :].reshape(10, 8, LANES)
        other = source_v[pl.ds(160 * pair + 80, 80), :].reshape(10, 8, LANES)
        even, odd = pair_up(first, other)
        lanes = pl.ds(pair * LANES, LANES)
        for p in range(10):
            rhs[2 * p, :, lanes] = even[p] * live
            rhs[2 * p + 1, :, lanes] = odd[p] * live

    def precondition(value, target):
        solved = times(mass_weights[...], value.reshape(FIELD, 2 * LANES))
        target[...] = solved.reshape(NODES, 8, 2 * LANES) * inv_denom[None]

    def fill_table(field):
        high, low = split(field[...])
        for h, part in enumerate((high, low)):
            for pair in range(2):
                block = jnp.concatenate(
                    [
                        jnp.concatenate(
                            [
                                part[FACE_NODE[t][f], :, pair * LANES : (pair + 1) * LANES]
                                for f in range(FACES)
                            ],
                            axis=1,
                        )
                        for t in range(TRI)
                    ],
                    axis=0,
                )
                table[pl.ds(h * ROWS + pair * 80, 80), :] = block.astype(BF16)

    group_of = iota((PART, LANES), 1) // SLOTS

    def trade_copies(trade):
        return [
            remote(
                outgoing.at[trade, place],
                incoming.at[trade, place],
                send_sem.at[trade, place],
                recv_sem.at[trade, place],
                targets[place],
            )
            for place in range(PEERS)
        ]

    trades = [trade_copies(0), trade_copies(1)]

    def send_traces(trade):
        for half in range(2):
            both = dot(table[...], pick_send[half])
            packed = both[:ROWS] + both[ROWS:]
            parts = [packed[j * PART : (j + 1) * PART] for j in range(4)]
            for g in range(4):
                message = None
                for j in range(4):
                    shift = (j - g) * SLOTS % LANES
                    part = pltpu.roll(parts[j], shift, 1) if shift else parts[j]
                    message = part if message is None else jnp.where(group_of == j, part, message)
                outgoing[trade, half * 4 + g] = message
            for place in range(half * 4, half * 4 + 4):
                pl.when(inside(targets[place]))(trades[trade][place].start)

    def receive_traces(trade):
        for place, copy in enumerate(trades[trade]):
            pl.when(inside(origins[place]))(copy.wait_recv)
        blocks = []
        for j in range(4):
            halves = []
            for half in range(2):
                gathered = None
                for g in range(4):
                    shift = (g - j) * SLOTS % LANES
                    part = incoming[trade, half * 4 + g]
                    part = pltpu.roll(part, shift, 1) if shift else part
                    gathered = part if gathered is None else jnp.where(group_of == g, part, gathered)
                halves.append(gathered)
            blocks.append(jnp.concatenate(halves, axis=1))
        received = jnp.concatenate(blocks, axis=0)
        high, low = split(received)
        return jnp.concatenate([high, low], axis=0).astype(BF16)

    precondition(rhs[...], direction)
    fill_table(direction)
    pl.when(is_early)(send_up)
    send_traces(0)

    flux = jnp.zeros(square, F32)
    for d in range(3):
        ahead = thrice(stiffness_v[d])
        back = thrice(stiffness_v[d].T)
        from_flux = (row_of % 8) + (d + 1) == lane_of % 8
        from_flux = jnp.logical_and(from_flux, row_of % 4 == 0)
        to_flux = (lane_of % 8) + (d + 1) == row_of % 8
        to_flux = jnp.logical_and(to_flux, lane_of % 4 == 0)
        flux = jnp.where(from_flux, dot(dot(rows, ahead).astype(BF16), columns), flux)
        flux = jnp.where(to_flux, dot(dot(rows, back).astype(BF16), columns), flux)
    flux_weights[...] = flux.astype(BF16)

    geo_in = jnp.where(sub % 4 == 0, 1.0, 0.0)
    geo_out = geo_in
    for d in range(3):
        here = sub % 4 == d + 1
        geo_in = jnp.where(here, geometry_v[d : d + 1, :], geo_in)
        geo_out = jnp.where(here, -geometry_v[d : d + 1, :], geo_out)
    geo_in = jnp.concatenate([geo_in, geo_in], axis=1)
    geo_out = jnp.concatenate([geo_out, geo_out], axis=1)

    pen_node = []
    for node in range(NODES):
        value = None
        for t in range(TRI):
            for f in range(FACES):
                if FACE_NODE[t][f] == node:
                    value = pen[f] if value is None else value + pen[f]
        pen_node.append(jnp.concatenate([value, value], axis=1))
    pen_row = jnp.concatenate(pen, axis=1)
    orient_row = jnp.concatenate([orient_v[f : f + 1, :] for f in range(FACES)], axis=1)

    def apply_local(field):
        both = dot(table[...], pick_local[...])
        value = field[...]
        flux_term = times(flux_weights[...], (value * geo_in[None]).reshape(FIELD, 2 * LANES))
        return both[:ROWS] + both[ROWS:], flux_term.reshape(NODES, 8, 2 * LANES)

    def apply_remote(field, solved, local, received, target):
        near, flux_term = local
        both = dot(received, pick_remote[...])
        across = near + both[:ROWS] + both[ROWS:]
        total = [None] * NODES
        for t in range(TRI):
            sides = []
            for pair in range(2):
                def rows_of(node):
                    start = pair * 80 + node * 8
                    return across[start : start + 8]

                side = rows_of(TURNED[0][t])
                for o in range(1, 6):
                    if TURNED[o][t] != TURNED[0][t]:
                        side = jnp.where(orient_row == o, rows_of(TURNED[o][t]), side)
                sides.append(side * pen_row)
            for f in range(FACES):
                lanes = slice(f * LANES, (f + 1) * LANES)
                jump = jnp.concatenate([side[:, lanes] for side in sides], axis=1)
                node = FACE_NODE[t][f]
                total[node] = jump if total[node] is None else total[node] + jump
        for node in range(NODES):
            value = ratio * solved[node] + geo_out * flux_term[node]
            value = value + pen_node[node] * field[node] - total[node]
            target[node] = live_two * value

    across = [
        [
            remote(
                level.at[step],
                along_in.at[first + k],
                along_send.at[first + k],
                along_recv.at[first + k],
                target,
            )
            for k, target in enumerate(line)
        ]
        for step, (first, line) in enumerate(((0, along_x), (len(along_x), along_y)))
    ]
    down = {
        z: [
            remote(top, top, down_send.at[i], down_recv.at[0], device(at_x, at_y, to, core))
            for i, to in enumerate(to for to in DOWN[z] if to < size_z)
        ]
        for z in planes
    }
    relays = [
        remote(top, top, down_send.at[i], down_recv.at[0], device(at_x, at_y, at_z + i + 1, core))
        for i in range(CUBE - 1)
    ]

    def column_slot(slot):
        return remote(own_best, column_in.at[slot], up_send.at[0], up_recv.at[slot], me + 1 - 2 * core)

    def meet_column():
        column_in[mine] = own_best[...]
        for k in range(1, size_z):
            for c in range(2):
                column_slot(lax.rem(at_z + k, size_z) * 2 + c).wait_recv()
        column_slot(at_z * 2 + 1 - core).wait_recv()
        level[0] = jnp.max(column_in[...], axis=0)
        for copy in across[0]:
            copy.start()

    def meet_line(step, first):
        value = level[step]
        for k, copy in enumerate(across[step]):
            copy.wait_recv()
            value = jnp.maximum(value, along_in[first + k])
        return value

    def meet_x():
        level[1] = meet_line(0, 0)
        for copy in across[1]:
            copy.start()

    def meet_y():
        top[...] = meet_line(1, len(along_x))
        for z in planes:

            @pl.when(at_z == z)
            def _(z=z):
                for copy in down[z]:
                    copy.start()

    local = apply_local(direction)
    pl.when(is_head)(meet_column)
    apply_remote(direction, rhs, local, receive_traces(0), applied)
    precondition(applied[...], second)
    fill_table(second)
    send_traces(1)
    pl.when(is_head)(meet_x)
    local = apply_local(second)
    pl.when(is_head)(meet_y)
    apply_remote(second, applied, local, receive_traces(1), twice)
    pl.when(jnp.logical_not(is_head))(down[0][0].wait_recv)

    @pl.when(is_relay)
    def _():
        for copy in relays:
            copy.start()

    upper = jnp.max(top[...], axis=1, keepdims=True)
    lower = 0.1 * upper
    centre = (upper + lower) / 2.0
    half_width = (upper - lower) / 2.0
    sigma_one = centre / half_width
    ratio_now = 1.0 / sigma_one
    ratio_new = 1.0 / (2.0 * sigma_one - ratio_now)
    inv_centre = 1.0 / centre
    step = 2.0 * ratio_new / half_width
    first_weight = inv_centre + ratio_new * ratio_now * inv_centre + step
    second_weight = -step * inv_centre
    sol = first_weight * direction[...] + second_weight * second[...]
    res = rhs[...] - first_weight * applied[...] - second_weight * twice[...]
    for value, target in ((sol, solution_out), (res, residual_out)):
        for pair in range(2):
            lanes = slice(pair * LANES, (pair + 1) * LANES)
            for p in range(10):
                even, odd = value[2 * p, :, lanes], value[2 * p + 1, :, lanes]
                low, high = pair_up(even[None], odd[None])
                target[pl.ds(160 * pair + 8 * p, 8), :] = low[0]
                target[pl.ds(160 * pair + 80 + 8 * p, 8), :] = high[0]

    for copies in trades:
        for place, copy in enumerate(copies):
            pl.when(inside(targets[place]))(copy.wait_send)
    for wanted, copy in zip(up_to, up):
        pl.when(wanted)(copy.wait_send)

    @pl.when(is_head)
    def _():
        for copy in across[0] + across[1]:
            copy.wait_send()

    for z in planes:

        @pl.when(at_z == z)
        def _(z=z):
            for copy in down[z]:
                copy.wait_send()

    @pl.when(is_relay)
    def _():
        for copy in relays:
            copy.wait_send()


def solution(mesh):
    n = mesh.shape["dom"]
    size_x, size_y, size_z = torus(n)
    along = max(size_x + size_y - 2, 1)

    def body(
        source, absorption, geometry, penalty, link, orient, send_index, live_count, mass, stiffness
    ):
        flat = source.transpose(0, 2, 1, 3).reshape(GASES * NODES * COMPS, LANES)
        operands = (
            flat,
            absorption,
            geometry,
            penalty,
            link,
            orient,
            send_index,
            live_count,
            mass,
            stiffness,
        )
        vmem = pltpu.VMEM
        field = vmem((NODES, 8, 2 * LANES), F32)
        dma = pltpu.SemaphoreType.DMA
        outs = pl.pallas_call(
            functools.partial(kernel, n),
            out_shape=[jax.ShapeDtypeStruct(flat.shape, F32)] * 2,
            in_specs=[pl.BlockSpec(memory_space=pltpu.HBM)] * 10,
            out_specs=[pl.BlockSpec(memory_space=vmem)] * 2,
            scratch_shapes=[
                vmem((320, LANES), F32),
                vmem((4, LANES), F32),
                vmem((3, LANES), F32),
                vmem((4, LANES), F32),
                vmem((4, LANES), jnp.int32),
                vmem((4, LANES), jnp.int32),
                vmem((1, PEERS, SLOTS), jnp.int32),
                pltpu.SMEM((1,), jnp.int32),
                vmem((NODES, NODES), F32),
                vmem((3, NODES, NODES), F32),
                field,
                field,
                field,
                field,
                field,
                vmem((FIELD, 3 * FIELD), BF16),
                vmem((FIELD, 3 * FIELD), BF16),
                vmem((2, LOCAL, LANES), BF16),
                vmem((LOCAL, LOCAL), BF16),
                vmem((REMOTE, LOCAL), BF16),
                vmem((2 * ROWS, LOCAL), BF16),
                vmem((2, PEERS, PART, LANES), F32),
                vmem((2, PEERS, PART, LANES), F32),
                vmem((1, LANES), F32),
                vmem((2 * size_z, 1, LANES), F32),
                vmem((along, 1, LANES), F32),
                vmem((2, 1, LANES), F32),
                vmem((1, LANES), F32),
                dma((10,)),
                dma((2, PEERS)),
                dma((2, PEERS)),
                dma((2 * len(DOWN),)),
                dma((2 * size_z,)),
                dma((along,)),
                dma((along,)),
                dma((6,)),
                dma((1,)),
            ],
            compiler_params=pltpu.CompilerParams(
                collective_id=0, has_side_effects=True, vmem_limit_bytes=32 * 2**20
            ),
            cost_estimate=pl.CostEstimate(
                flops=2_000_000_000, bytes_accessed=1_000_000, transcendentals=0
            ),
        )(*[
                value if value is live_count else pltpu.with_memory_space_constraint(value, pltpu.HBM)
                for value in operands
            ]
        )
        return tuple(
            out.reshape(GASES, NODES, COMPS, LANES).transpose(0, 2, 1, 3) for out in outs
        )

    in_specs = (
        P(None, None, None, "dom"),
        P(None, "dom"),
        P(None, "dom"),
        P(None, "dom"),
        P(None, "dom"),
        P(None, "dom"),
        P("dom", None, None),
        P("dom"),
        P(),
        P(),
    )
    out_specs = (P(None, None, None, "dom"), P(None, None, None, "dom"))
    return jax.shard_map(body, mesh=mesh, in_specs=in_specs, out_specs=out_specs, check_vma=False)
```

```python
import functools

import jax
import jax.numpy as jnp
import numpy as np
from jax import lax
from jax.experimental import pallas as pl
from jax.experimental.pallas import tpu as pltpu
from jax.sharding import PartitionSpec as P

MESH = pl.DeviceIdType.MESH
F32 = jnp.float32
BF16 = jnp.bfloat16
GASES = 4
COMPS = 4
NODES = 20
FACES = 4
TRI = 10
SLOTS = 32
PEERS = 8
LANES = 128
OFFSETS = tuple(q + 1 if q < 4 else -(q - 3) for q in range(PEERS))
LOCAL = FACES * LANES
REMOTE = PEERS * SLOTS
ROWS = 2 * TRI * 8
PART = ROWS // 4
FIELD = NODES * 8


def node_tables():
    triangle = [(a, b, 3 - a - b) for a in range(4) for b in range(4 - a)]
    tetra_nodes = [
        (i, j, k, 3 - i - j - k) for i in range(4) for j in range(4 - i) for k in range(4 - i - j)
    ]
    face_index = np.zeros((10, 4), np.int32)
    for t in range(10):
        for f in range(4):
            coords = list(triangle[t])
            coords.insert(f, 0)
            face_index[t, f] = tetra_nodes.index(tuple(coords))
    orders = ((0, 1, 2), (1, 2, 0), (2, 0, 1), (0, 2, 1), (2, 1, 0), (1, 0, 2))
    turned = np.zeros((6, 10), np.int32)
    for o in range(6):
        for t in range(10):
            turned[o, t] = triangle.index(tuple((triangle[t][q] for q in orders[o])))
    return face_index.tolist(), turned.tolist()


FACE_NODE, TURNED = node_tables()


ORDER = (3, 7, 2, 6, 1, 5, 0, 4)
NEAR, FAR = 0, 4
DOWN = {NEAR: (1, 2, 12, 3, 13, 14, 15), FAR: (8, 11, 10, 9, 5, 6, 7)}
EARLY = 4


def torus(count):
    chips = count // 2
    z = 16 if chips >= 256 else min(chips, 4)
    y = min(4, chips // z)
    return chips // (z * y), y, z


def iota(shape, axis):
    return lax.broadcasted_iota(jnp.int32, shape, axis)


def split(value):
    high = value.astype(BF16).astype(F32)
    return high, value - high


def dot(a, b):
    return jnp.dot(a, b, preferred_element_type=F32)


def invert(matrix):
    size = matrix.shape[0]
    lane, sub = iota((size, LANES), 1), iota((size, LANES), 0)
    planes = [jnp.broadcast_to(matrix[:, i : i + 1], (size, LANES)) for i in range(size)]
    state = jnp.stack(planes, axis=0)
    for k in range(size):
        pivot = 1.0 / state[k, k : k + 1]
        row = state[k] * pivot
        change = jnp.where(sub == k, 1.0 + pivot, row)
        row = jnp.where(sub == k, pivot, row)
        rest = state - state[:, k : k + 1, :] * change[None]
        state = jnp.concatenate(
            [part for part in (rest[:k], row[None], rest[k + 1 :]) if part.shape[0]], axis=0
        )
    inverse = state[0]
    for i in range(1, size):
        inverse = jnp.where(lane == i, state[i], inverse)
    return inverse[:, :size]


def spread_rows():
    return (iota((FIELD, NODES), 0) // 8 == iota((FIELD, NODES), 1)).astype(F32).astype(BF16)


def spread_columns():
    shape = (3 * NODES, 3 * FIELD)
    return (iota(shape, 1) // 8 == iota(shape, 0)).astype(F32).astype(BF16)


def thrice(matrix):
    high, low = split(matrix)
    return jnp.concatenate([high, high, low], axis=1).astype(BF16)


def times(weights, field):
    high, low = split(field)
    return dot(weights, jnp.concatenate([high, low, high], axis=0).astype(BF16))


def pair_up(first, second):
    sub = iota(first.shape, 1)
    even = jnp.where(sub < 4, first, pltpu.roll(second, 4, 1))
    odd = jnp.where(sub < 4, pltpu.roll(first, 4, 1), second)
    return even, odd


def kernel(
    n,
    source,
    absorption,
    geometry,
    penalty,
    link,
    orient,
    send_index,
    live_count,
    mass,
    stiffness,
    direction_out,
    second_out,
    rhs_out,
    applied_out,
    twice_out,
    weights_out,
    source_v,
    absorption_v,
    geometry_v,
    penalty_v,
    link_v,
    orient_v,
    send_v,
    live_v,
    mass_v,
    stiffness_v,
    rhs,
    direction,
    applied,
    second,
    twice,
    mass_weights,
    flux_weights,
    pick_send,
    pick_local,
    pick_remote,
    table,
    outgoing,
    incoming,
    own_best,
    column_in,
    along_in,
    level,
    top,
    in_sem,
    send_sem,
    recv_sem,
    up_send,
    up_recv,
    along_send,
    along_recv,
    down_send,
    down_recv,
):
    me = lax.axis_index("dom")
    size_x, size_y, size_z = torus(n)
    core = lax.rem(me, 2)
    at_z = lax.rem(me // 2, size_z)
    at_y = lax.rem(me // (2 * size_z), size_y)
    at_x = me // (2 * size_z * size_y)

    def device(x, y, z, c):
        return ((x * size_y + y) * size_z + z) * 2 + c

    def inside(index):
        return jnp.logical_and(index >= 0, index < n)

    targets = [me + OFFSETS[q] for q in ORDER]
    origins = [me - OFFSETS[q] for q in ORDER]
    along_x = [device(lax.rem(at_x + k, size_x), at_y, at_z, core) for k in range(1, size_x)]
    along_y = [device(at_x, lax.rem(at_y + k, size_y), at_z, core) for k in range(1, size_y)]
    is_near = at_z == NEAR
    is_far = at_z == FAR
    has_far = FAR < size_z
    is_early = at_z < EARLY

    barrier = pltpu.get_barrier_semaphore()

    def greet(target):
        pl.semaphore_signal(barrier, inc=1, device_id=(target,), device_id_type=MESH)

    loads = []
    for i, (src, dst) in enumerate(
        (
            (penalty, penalty_v),
            (live_count, live_v),
            (mass, mass_v),
            (send_index, send_v),
            (source, source_v),
            (absorption, absorption_v),
            (geometry, geometry_v),
            (link, link_v),
            (orient, orient_v),
            (stiffness, stiffness_v),
        )
    ):
        loads.append(pltpu.make_async_copy(src, dst, in_sem.at[i]))
    for copy in loads[:3]:
        copy.start()
    for target in targets:
        pl.when(inside(target))(functools.partial(greet, target))

    def greet_all(sources, place):
        def one(k, carry):
            target = place(k)
            pl.when(target != me)(functools.partial(greet, target))
            return carry

        lax.fori_loop(0, sources, one, 0)

    for copy in loads[3:]:
        copy.start()
    column = 2 * size_z

    @pl.when(is_near)
    def _():
        for target in along_y:
            greet(target)
        greet_all(
            size_x * column, lambda k: (k // column * size_y + at_y) * column + lax.rem(k, column)
        )

    if has_far:

        @pl.when(is_far)
        def _():
            for target in along_x + along_y:
                greet(target)
            greet_all(column, lambda k: (at_x * size_y + at_y) * column + k)

    for copy in loads[:2]:
        copy.wait()
    live = (iota((1, LANES), 1) < live_v[0]).astype(F32)
    pen = [penalty_v[f : f + 1, :] for f in range(FACES)]
    pen_sum = pen[0] + pen[1] + pen[2] + pen[3]
    best = jnp.where(live > 0.5, 1.0 + 0.25 * pen_sum, 0.0)
    own_best[...] = best

    def remote(src, dst, send, recv, target):
        return pltpu.make_async_remote_copy(
            src_ref=src,
            dst_ref=dst,
            send_sem=send,
            recv_sem=recv,
            device_id=(target,),
            device_id_type=MESH,
        )

    mine = at_z * 2 + core
    slots = [((at_x * size_z + at_z) * 2 + core, NEAR, x) for x in range(size_x)]
    if has_far:
        slots.insert(1, (mine, FAR, at_x))
    up, up_to = [], []
    for slot, z, x in slots:
        for c in range(2):
            target = device(x, at_y, z, c)
            up.append(
                remote(own_best, column_in.at[slot], up_send.at[len(up)], up_recv.at[0], target)
            )
            up_to.append(target != me)
    partners = sum([inside(target).astype(jnp.int32) for target in targets])
    partners = partners + sum([wanted.astype(jnp.int32) for wanted in up_to])
    partners = partners + is_near.astype(jnp.int32) * len(along_y)
    partners = partners + is_far.astype(jnp.int32) * (len(along_x) + len(along_y))

    def send_up():
        pl.semaphore_wait(barrier, partners)
        for wanted, copy in zip(up_to, up):
            pl.when(wanted)(copy.start)

    pl.when(jnp.logical_not(is_early))(send_up)

    for copy in loads[2:]:
        copy.wait()

    rows = spread_rows()
    columns = spread_columns()
    inverse = thrice(invert(mass_v[...]))
    square = (FIELD, 3 * FIELD)
    lane_of, row_of = iota(square, 1), iota(square, 0)
    wide = dot(dot(rows, inverse).astype(BF16), columns)
    mass_weights[...] = jnp.where(lane_of % 8 == row_of % 8, wide, 0.0).astype(BF16)

    sends = send_v[0]
    four = jnp.concatenate([sends, sends, sends, sends], axis=1)
    slot_q, slot_group = iota((PEERS, LANES), 0), iota((PEERS, LANES), 1) // SLOTS
    for half in range(2):
        wanted = jnp.zeros((PEERS, LANES), jnp.int32)
        for g in range(4):
            wanted = jnp.where(slot_group == g, ORDER[half * 4 + g], wanted)
        chosen = jnp.sum(jnp.where(slot_q == wanted, four, 0), axis=0, keepdims=True)
        pick = iota((LOCAL, LANES), 0) == chosen
        pick_send[half] = pick.astype(F32).astype(BF16)

    for f in range(FACES):
        lanes = pl.ds(f * LANES, LANES)
        wanted = link_v[f : f + 1, :]
        pick_local[:, lanes] = (iota((LOCAL, LANES), 0) == wanted).astype(F32).astype(BF16)
        for place, q in enumerate(ORDER):
            pick = iota((SLOTS, LANES), 0) + (LOCAL + q * SLOTS) == wanted
            pick_remote[pl.ds(place * SLOTS, SLOTS), lanes] = pick.astype(F32).astype(BF16)

    for place, origin in enumerate(origins):

        @pl.when(jnp.logical_not(inside(origin)))
        def _(place=place):
            for trade in range(2):
                incoming[trade, place] = jnp.zeros((PART, LANES), F32)

    sub = iota((8, LANES), 0)
    scale = jnp.where(sub % 4 == 0, 1.0, 3.0)
    coef = jnp.concatenate(
        [
            jnp.where(
                sub < 4,
                absorption_v[2 * pair : 2 * pair + 1, :],
                absorption_v[2 * pair + 1 : 2 * pair + 2, :],
            )
            * scale
            for pair in range(2)
        ],
        axis=1,
    )
    pen_sum_two = jnp.concatenate([pen_sum, pen_sum], axis=1)
    live_two = jnp.concatenate([live, live], axis=1)
    inv_denom = 1.0 / (coef + 0.5 * pen_sum_two)
    ratio = coef * inv_denom

    for pair in range(2):
        first = source_v[pl.ds(160 * pair, 80), :].reshape(10, 8, LANES)
        other = source_v[pl.ds(160 * pair + 80, 80), :].reshape(10, 8, LANES)
        even, odd = pair_up(first, other)
        lanes = pl.ds(pair * LANES, LANES)
        for p in range(10):
            rhs[2 * p, :, lanes] = even[p] * live
            rhs[2 * p + 1, :, lanes] = odd[p] * live

    def precondition(value, target):
        solved = times(mass_weights[...], value.reshape(FIELD, 2 * LANES))
        target[...] = solved.reshape(NODES, 8, 2 * LANES) * inv_denom[None]

    def fill_table(field):
        high, low = split(field[...])
        for h, part in enumerate((high, low)):
            for pair in range(2):
                block = jnp.concatenate(
                    [
                        jnp.concatenate(
                            [
                                part[FACE_NODE[t][f], :, pair * LANES : (pair + 1) * LANES]
                                for f in range(FACES)
                            ],
                            axis=1,
                        )
                        for t in range(TRI)
                    ],
                    axis=0,
                )
                table[pl.ds(h * ROWS + pair * 80, 80), :] = block.astype(BF16)

    group_of = iota((PART, LANES), 1) // SLOTS

    def trade_copies(trade):
        return [
            remote(
                outgoing.at[trade, place],
                incoming.at[trade, place],
                send_sem.at[trade, place],
                recv_sem.at[trade, place],
                targets[place],
            )
            for place in range(PEERS)
        ]

    trades = [trade_copies(0), trade_copies(1)]

    def send_traces(trade):
        for half in range(2):
            both = dot(table[...], pick_send[half])
            packed = both[:ROWS] + both[ROWS:]
            parts = [packed[j * PART : (j + 1) * PART] for j in range(4)]
            for g in range(4):
                message = None
                for j in range(4):
                    shift = (j - g) * SLOTS % LANES
                    part = pltpu.roll(parts[j], shift, 1) if shift else parts[j]
                    message = part if message is None else jnp.where(group_of == j, part, message)
                outgoing[trade, half * 4 + g] = message
            for place in range(half * 4, half * 4 + 4):
                pl.when(inside(targets[place]))(trades[trade][place].start)

    def receive_traces(trade, near):
        for half in range(2):
            for place in range(half * 4, half * 4 + 4):
                pl.when(inside(origins[place]))(trades[trade][place].wait_recv)
            blocks = []
            for j in range(4):
                gathered = None
                for g in range(4):
                    shift = (g - j) * SLOTS % LANES
                    part = incoming[trade, half * 4 + g]
                    part = pltpu.roll(part, shift, 1) if shift else part
                    gathered = part if gathered is None else jnp.where(group_of == g, part, gathered)
                blocks.append(gathered)
            high, low = split(jnp.concatenate(blocks, axis=0))
            received = jnp.concatenate([high, low], axis=0).astype(BF16)
            both = dot(received, pick_remote[pl.ds(half * LANES, LANES), :])
            near = near + (both[:ROWS] + both[ROWS:])
        return near

    precondition(rhs[...], direction)
    fill_table(direction)
    pl.when(is_early)(send_up)
    send_traces(0)

    flux = jnp.zeros(square, F32)
    for d in range(3):
        ahead = thrice(stiffness_v[d])
        back = thrice(stiffness_v[d].T)
        from_flux = (row_of % 8) + (d + 1) == lane_of % 8
        from_flux = jnp.logical_and(from_flux, row_of % 4 == 0)
        to_flux = (lane_of % 8) + (d + 1) == row_of % 8
        to_flux = jnp.logical_and(to_flux, lane_of % 4 == 0)
        flux = jnp.where(from_flux, dot(dot(rows, ahead).astype(BF16), columns), flux)
        flux = jnp.where(to_flux, dot(dot(rows, back).astype(BF16), columns), flux)
    flux_weights[...] = flux.astype(BF16)

    geo_in = jnp.where(sub % 4 == 0, 1.0, 0.0)
    geo_out = geo_in
    for d in range(3):
        here = sub % 4 == d + 1
        geo_in = jnp.where(here, geometry_v[d : d + 1, :], geo_in)
        geo_out = jnp.where(here, -geometry_v[d : d + 1, :], geo_out)
    geo_in = jnp.concatenate([geo_in, geo_in], axis=1)
    geo_out = jnp.concatenate([geo_out, geo_out], axis=1)

    pen_node = []
    for node in range(NODES):
        value = None
        for t in range(TRI):
            for f in range(FACES):
                if FACE_NODE[t][f] == node:
                    value = pen[f] if value is None else value + pen[f]
        pen_node.append(jnp.concatenate([value, value], axis=1))
    pen_row = jnp.concatenate(pen, axis=1)
    orient_row = jnp.concatenate([orient_v[f : f + 1, :] for f in range(FACES)], axis=1)

    def apply_local(field):
        both = dot(table[...], pick_local[...])
        value = field[...]
        flux_term = times(flux_weights[...], (value * geo_in[None]).reshape(FIELD, 2 * LANES))
        return both[:ROWS] + both[ROWS:], flux_term.reshape(NODES, 8, 2 * LANES)

    def apply_remote(trade, field, solved, local, target):
        near, flux_term = local
        across = receive_traces(trade, near)
        total = [None] * NODES
        for t in range(TRI):
            sides = []
            for pair in range(2):
                def rows_of(node):
                    start = pair * 80 + node * 8
                    return across[start : start + 8]

                side = rows_of(TURNED[0][t])
                for o in range(1, 6):
                    if TURNED[o][t] != TURNED[0][t]:
                        side = jnp.where(orient_row == o, rows_of(TURNED[o][t]), side)
                sides.append(side * pen_row)
            for f in range(FACES):
                lanes = slice(f * LANES, (f + 1) * LANES)
                jump = jnp.concatenate([side[:, lanes] for side in sides], axis=1)
                node = FACE_NODE[t][f]
                total[node] = jump if total[node] is None else total[node] + jump
        for node in range(NODES):
            value = ratio * solved[node] + geo_out * flux_term[node]
            value = value + pen_node[node] * field[node] - total[node]
            target[node] = live_two * value

    across_x, across_y = [
        [
            remote(
                level.at[step],
                along_in.at[first + k],
                along_send.at[first + k],
                along_recv.at[first + k],
                target,
            )
            for k, target in enumerate(line)
        ]
        for step, (first, line) in enumerate(((0, along_x), (len(along_x), along_y)))
    ]

    def down(plane):
        return [
            remote(top, top, down_send.at[i], down_recv.at[0], device(at_x, at_y, z, core))
            for i, z in enumerate(z for z in DOWN[plane] if z < size_z)
        ]

    def meet_column(count, own, step, copies):
        column_in[own] = own_best[...]
        pltpu.make_async_copy(
            column_in.at[pl.ds(0, count - 1)], column_in.at[pl.ds(0, count - 1)], up_recv.at[0]
        ).wait()
        level[step] = jnp.max(column_in[pl.ds(0, count)], axis=0)
        for copy in copies:
            copy.start()

    def meet_line(step, first, copies):
        value = level[step]
        for k, copy in enumerate(copies):
            copy.wait_recv()
            value = jnp.maximum(value, along_in[first + k])
        return value

    def meet_near():
        meet_column(size_x * column, (at_x * size_z + at_z) * 2 + core, 1, across_y)

    def meet_far():
        meet_column(column, mine, 0, across_x)

    def meet_x():
        level[1] = meet_line(0, 0, across_x)
        for copy in across_y:
            copy.start()

    def meet_y(plane):
        top[...] = meet_line(1, len(along_x), across_y)
        for copy in down(plane):
            copy.start()

    def wait_all(copies):
        for copy in copies:
            copy.wait_send()

    def write_out(field, target):
        value = field[...]
        for pair in range(2):
            lanes = slice(pair * LANES, (pair + 1) * LANES)
            for p in range(10):
                even, odd = value[2 * p, :, lanes], value[2 * p + 1, :, lanes]
                low, high = pair_up(even[None], odd[None])
                target[pl.ds(160 * pair + 8 * p, 8), :] = low[0]
                target[pl.ds(160 * pair + 80 + 8 * p, 8), :] = high[0]

    local = apply_local(direction)
    pl.when(is_near)(meet_near)
    if has_far:
        pl.when(is_far)(meet_far)
    apply_remote(0, direction, rhs, local, applied)
    precondition(applied[...], second)
    fill_table(second)
    send_traces(1)
    if has_far:
        pl.when(is_far)(meet_x)
    local = apply_local(second)
    for field, target in (
        (direction, direction_out),
        (second, second_out),
        (rhs, rhs_out),
        (applied, applied_out),
    ):
        write_out(field, target)
    pl.when(is_near)(functools.partial(meet_y, NEAR))
    if has_far:
        pl.when(is_far)(functools.partial(meet_y, FAR))
    apply_remote(1, second, applied, local, twice)
    write_out(twice, twice_out)
    is_head = jnp.logical_or(is_near, is_far)
    pl.when(jnp.logical_not(is_head))(down(NEAR)[0].wait_recv)

    upper = jnp.max(top[...], axis=1, keepdims=True)
    lower = 0.1 * upper
    centre = (upper + lower) / 2.0
    half_width = (upper - lower) / 2.0
    sigma_one = centre / half_width
    ratio_now = 1.0 / sigma_one
    ratio_new = 1.0 / (2.0 * sigma_one - ratio_now)
    inv_centre = 1.0 / centre
    step = 2.0 * ratio_new / half_width
    first_weight = inv_centre + ratio_new * ratio_now * inv_centre + step
    second_weight = -step * inv_centre
    weights_out[0:1, :] = jnp.broadcast_to(first_weight, (1, LANES))
    weights_out[1:2, :] = jnp.broadcast_to(second_weight, (1, LANES))

    for copies in trades:
        for place, copy in enumerate(copies):
            pl.when(inside(targets[place]))(copy.wait_send)
    for wanted, copy in zip(up_to, up):
        pl.when(wanted)(copy.wait_send)
    pl.when(is_near)(functools.partial(wait_all, across_y + down(NEAR)))
    if has_far:
        pl.when(is_far)(functools.partial(wait_all, across_x + across_y + down(FAR)))


def solution(mesh):
    n = mesh.shape["dom"]
    size_x, size_y, size_z = torus(n)
    along = max(size_x + size_y - 2, 1)

    def body(
        source, absorption, geometry, penalty, link, orient, send_index, live_count, mass, stiffness
    ):
        flat = source.transpose(0, 2, 1, 3).reshape(GASES * NODES * COMPS, LANES)
        operands = (
            flat,
            absorption,
            geometry,
            penalty,
            link,
            orient,
            send_index,
            live_count,
            mass,
            stiffness,
        )
        vmem = pltpu.VMEM
        field = vmem((NODES, 8, 2 * LANES), F32)
        dma = pltpu.SemaphoreType.DMA
        first, second, rhs, applied, twice, weights = pl.pallas_call(
            functools.partial(kernel, n),
            out_shape=[jax.ShapeDtypeStruct(flat.shape, F32)] * 5
            + [jax.ShapeDtypeStruct((2, LANES), F32)],
            in_specs=[pl.BlockSpec(memory_space=pltpu.HBM)] * 10,
            out_specs=[pl.BlockSpec(memory_space=vmem)] * 6,
            scratch_shapes=[
                vmem((320, LANES), F32),
                vmem((4, LANES), F32),
                vmem((3, LANES), F32),
                vmem((4, LANES), F32),
                vmem((4, LANES), jnp.int32),
                vmem((4, LANES), jnp.int32),
                vmem((1, PEERS, SLOTS), jnp.int32),
                pltpu.SMEM((1,), jnp.int32),
                vmem((NODES, NODES), F32),
                vmem((3, NODES, NODES), F32),
                field,
                field,
                field,
                field,
                field,
                vmem((FIELD, 3 * FIELD), BF16),
                vmem((FIELD, 3 * FIELD), BF16),
                vmem((2, LOCAL, LANES), BF16),
                vmem((LOCAL, LOCAL), BF16),
                vmem((REMOTE, LOCAL), BF16),
                vmem((2 * ROWS, LOCAL), BF16),
                vmem((2, PEERS, PART, LANES), F32),
                vmem((2, PEERS, PART, LANES), F32),
                vmem((1, LANES), F32),
                vmem((2 * size_z * size_x, 1, LANES), F32),
                vmem((along, 1, LANES), F32),
                vmem((2, 1, LANES), F32),
                vmem((1, LANES), F32),
                dma((10,)),
                dma((2, PEERS)),
                dma((2, PEERS)),
                dma((2 * size_x + 2,)),
                dma((1,)),
                dma((along,)),
                dma((along,)),
                dma((7,)),
                dma((1,)),
            ],
            compiler_params=pltpu.CompilerParams(
                collective_id=0, has_side_effects=True, vmem_limit_bytes=32 * 2**20
            ),
            cost_estimate=pl.CostEstimate(
                flops=2_000_000_000, bytes_accessed=1_000_000, transcendentals=0
            ),
        )(*[
                value if value is live_count else pltpu.with_memory_space_constraint(value, pltpu.HBM)
                for value in operands
            ]
        )
        outs = (
            weights[0] * first + weights[1] * second,
            rhs - weights[0] * applied - weights[1] * twice,
        )
        return tuple(
            out.reshape(GASES, NODES, COMPS, LANES).transpose(0, 2, 1, 3) for out in outs
        )

    in_specs = (
        P(None, None, None, "dom"),
        P(None, "dom"),
        P(None, "dom"),
        P(None, "dom"),
        P(None, "dom"),
        P(None, "dom"),
        P("dom", None, None),
        P("dom"),
        P(),
        P(),
    )
    out_specs = (P(None, None, None, "dom"), P(None, None, None, "dom"))
    return jax.shard_map(body, mesh=mesh, in_specs=in_specs, out_specs=out_specs, check_vma=False)
```

```python
import functools

import jax
import jax.numpy as jnp
import numpy as np
from jax import lax
from jax.experimental import pallas as pl
from jax.experimental.pallas import tpu as pltpu
from jax.sharding import PartitionSpec as P

MESH = pl.DeviceIdType.MESH
F32 = jnp.float32
BF16 = jnp.bfloat16
GASES = 4
COMPS = 4
NODES = 20
FACES = 4
TRI = 10
SLOTS = 32
PEERS = 8
LANES = 128
OFFSETS = tuple(q + 1 if q < 4 else -(q - 3) for q in range(PEERS))
LOCAL = FACES * LANES
REMOTE = PEERS * SLOTS
ROWS = 2 * TRI * 8
PART = ROWS // 4
FIELD = NODES * 8


def node_tables():
    triangle = [(a, b, 3 - a - b) for a in range(4) for b in range(4 - a)]
    tetra_nodes = [
        (i, j, k, 3 - i - j - k) for i in range(4) for j in range(4 - i) for k in range(4 - i - j)
    ]
    face_index = np.zeros((10, 4), np.int32)
    for t in range(10):
        for f in range(4):
            coords = list(triangle[t])
            coords.insert(f, 0)
            face_index[t, f] = tetra_nodes.index(tuple(coords))
    orders = ((0, 1, 2), (1, 2, 0), (2, 0, 1), (0, 2, 1), (2, 1, 0), (1, 0, 2))
    turned = np.zeros((6, 10), np.int32)
    for o in range(6):
        for t in range(10):
            turned[o, t] = triangle.index(tuple((triangle[t][q] for q in orders[o])))
    return face_index.tolist(), turned.tolist()


FACE_NODE, TURNED = node_tables()


def step_weights():
    centre, half_width = (1.0 + 0.1) / 2.0, (1.0 - 0.1) / 2.0
    sigma_one = centre / half_width
    ratio = 1.0 / sigma_one
    ratio_new = 1.0 / (2.0 * sigma_one - ratio)
    step = 2.0 * ratio_new / half_width
    return (1.0 + ratio_new * ratio) / centre + step, -step / centre


FIRST_WEIGHT, SECOND_WEIGHT = step_weights()


ORDER = (7, 6, 5, 4, 3, 2, 1, 0)
DOWN = (4, 1, 5, 2, 3, 8, 12, 9, 10, 11)
RELAY = {4: (6, 7), 12: (13, 14, 15)}
REACH = 4
EARLY = 4


def torus(count):
    chips = count // 2
    z = 16 if chips >= 256 else min(chips, 4)
    y = min(4, chips // z)
    return chips // (z * y), y, z


def iota(shape, axis):
    return lax.broadcasted_iota(jnp.int32, shape, axis)


def split(value):
    high = value.astype(BF16).astype(F32)
    return high, value - high


def dot(a, b):
    return jnp.dot(a, b, preferred_element_type=F32)


def invert(matrix):
    size = matrix.shape[0]
    lane, sub = iota((size, LANES), 1), iota((size, LANES), 0)
    planes = [jnp.broadcast_to(matrix[:, i : i + 1], (size, LANES)) for i in range(size)]
    state = jnp.stack(planes, axis=0)
    for k in range(size):
        pivot = 1.0 / state[k, k : k + 1]
        row = state[k] * pivot
        change = jnp.where(sub == k, 1.0 + pivot, row)
        row = jnp.where(sub == k, pivot, row)
        rest = state - state[:, k : k + 1, :] * change[None]
        state = jnp.concatenate(
            [part for part in (rest[:k], row[None], rest[k + 1 :]) if part.shape[0]], axis=0
        )
    inverse = state[0]
    for i in range(1, size):
        inverse = jnp.where(lane == i, state[i], inverse)
    return inverse[:, :size]


def spread_rows():
    return (iota((FIELD, NODES), 0) // 8 == iota((FIELD, NODES), 1)).astype(F32).astype(BF16)


def spread_columns():
    shape = (3 * NODES, 3 * FIELD)
    return (iota(shape, 1) // 8 == iota(shape, 0)).astype(F32).astype(BF16)


def thrice(matrix):
    high, low = split(matrix)
    return jnp.concatenate([high, high, low], axis=1).astype(BF16)


def times(weights, field):
    high, low = split(field)
    return dot(weights, jnp.concatenate([high, low, high], axis=0).astype(BF16))


def pair_up(first, second):
    sub = iota(first.shape, 1)
    even = jnp.where(sub < 4, first, pltpu.roll(second, 4, 1))
    odd = jnp.where(sub < 4, pltpu.roll(first, 4, 1), second)
    return even, odd


def kernel(
    n,
    source,
    absorption,
    geometry,
    penalty_v,
    link,
    orient,
    send_index,
    live_count,
    mass,
    stiffness,
    direction_out,
    second_out,
    rhs_out,
    applied_out,
    twice_out,
    weights_out,
    source_v,
    absorption_v,
    geometry_v,
    link_v,
    orient_v,
    send_v,
    mass_v,
    stiffness_v,
    rhs,
    direction,
    applied,
    second,
    twice,
    mass_weights,
    flux_weights,
    pick_send,
    pick_local,
    pick_remote,
    table,
    outgoing,
    incoming,
    held,
    own_best,
    column_in,
    along_in,
    level,
    top,
    in_sem,
    send_sem,
    recv_sem,
    held_send,
    held_recv,
    up_send,
    up_recv,
    along_send,
    along_recv,
    down_send,
    down_recv,
):
    me = lax.axis_index("dom")
    size_x, size_y, size_z = torus(n)
    core = lax.rem(me, 2)
    at_z = lax.rem(me // 2, size_z)
    at_y = lax.rem(me // (2 * size_z), size_y)
    at_x = me // (2 * size_z * size_y)

    def device(x, y, z, c):
        return ((x * size_y + y) * size_z + z) * 2 + c

    def inside(index):
        return jnp.logical_and(index >= 0, index < n)

    targets = [me + OFFSETS[q] for q in ORDER]
    origins = [me - OFFSETS[q] for q in ORDER]
    along_x = [device(lax.rem(at_x + k, size_x), at_y, at_z, core) for k in range(1, size_x)]
    along_y = [device(at_x, lax.rem(at_y + k, size_y), at_z, core) for k in range(1, size_y)]
    is_head = at_z == 0
    is_early = at_z < EARLY

    column = 2 * size_z
    plane = column * size_y
    across_planes = size_x > 1 and size_z >= 4
    in_plane = lax.rem(me, plane)
    passed = in_plane - (plane - column)
    is_passing = jnp.logical_and(
        jnp.logical_and(passed >= 0, passed < REACH), jnp.logical_and(me + column < n, across_planes)
    )
    is_detoured = jnp.logical_and(
        in_plane < REACH, jnp.logical_and(me >= plane, across_planes)
    )

    def detours(reach):
        return jnp.logical_and(is_detoured, in_plane < reach)

    barrier = pltpu.get_barrier_semaphore()

    def greet(target):
        pl.semaphore_signal(barrier, inc=1, device_id=(target,), device_id_type=MESH)

    loads = []
    for i, (src, dst) in enumerate(
        (
            (mass, mass_v),
            (send_index, send_v),
            (source, source_v),
            (absorption, absorption_v),
            (geometry, geometry_v),
            (link, link_v),
            (orient, orient_v),
            (stiffness, stiffness_v),
        )
    ):
        loads.append(pltpu.make_async_copy(src, dst, in_sem.at[i]))
    loads[0].start()
    for reach in range(REACH, 0, -1):
        pl.when(inside(me - reach))(functools.partial(greet, me - reach))
        ahead = me + reach
        over = jnp.logical_and(in_plane + reach >= plane, across_planes)
        pl.when(inside(ahead))(functools.partial(greet, jnp.where(over, ahead - column, ahead)))
    pl.when(is_passing)(functools.partial(greet, me + column))

    for copy in loads[1:]:
        copy.start()
    @pl.when(is_head)
    def _():
        for z in sorted(range(1, size_z), key=lambda z: abs(z - size_z // 2 - 1)):
            for x in range(size_x):
                for c in range(2):
                    greet(device(x, at_y, z, c))
        greet(device(at_x, at_y, at_z, 1 - core))
        for target in along_x:
            for c in range(2):
                greet(target - core + c)
        for target in along_y:
            greet(target)

    live = (iota((1, LANES), 1) < live_count[0]).astype(F32)
    pen = [penalty_v[f : f + 1, :] for f in range(FACES)]
    pen_sum = pen[0] + pen[1] + pen[2] + pen[3]
    best = jnp.where(live > 0.5, 1.0 + 0.25 * pen_sum, 0.0)
    own_best[...] = best

    def remote(src, dst, send, recv, target):
        return pltpu.make_async_remote_copy(
            src_ref=src,
            dst_ref=dst,
            send_sem=send,
            recv_sem=recv,
            device_id=(target,),
            device_id_type=MESH,
        )

    mine = at_x * column + at_z * 2 + core
    up, up_to = [], []
    for x in range(size_x):
        for c in range(2):
            target = device(x, at_y, 0, c)
            up.append(
                remote(own_best, column_in.at[mine], up_send.at[len(up)], up_recv.at[0], target)
            )
            up_to.append(target != me)

    def count(wanted):
        return sum([each.astype(jnp.int32) for each in wanted])

    partners = count(up_to) + is_head.astype(jnp.int32) * len(along_y)
    partners = partners + count([inside(me + reach) for reach in range(1, REACH + 1)])
    partners = partners + count(
        [
            jnp.logical_and(inside(me - reach), jnp.logical_not(detours(reach)))
            for reach in range(1, REACH + 1)
        ]
    )
    partners = partners + is_detoured.astype(jnp.int32)
    partners = partners + is_passing.astype(jnp.int32) * (REACH - passed)

    def await_partners():
        pl.semaphore_wait(barrier, partners)

    def send_up():
        for wanted, copy in zip(up_to, up):
            pl.when(wanted)(copy.start)

    @pl.when(jnp.logical_not(is_early))
    def _():
        await_partners()
        send_up()

    for copy in loads:
        copy.wait()

    rows = spread_rows()
    columns = spread_columns()
    inverse = thrice(invert(mass_v[...]))
    square = (FIELD, 3 * FIELD)
    lane_of, row_of = iota(square, 1), iota(square, 0)
    wide = dot(dot(rows, inverse).astype(BF16), columns)
    mass_weights[...] = jnp.where(lane_of % 8 == row_of % 8, wide, 0.0).astype(BF16)

    sends = send_v[0]
    four = jnp.concatenate([sends, sends, sends, sends], axis=1)
    slot_q, slot_group = iota((PEERS, LANES), 0), iota((PEERS, LANES), 1) // SLOTS
    for half in range(2):
        wanted = jnp.zeros((PEERS, LANES), jnp.int32)
        for g in range(4):
            wanted = jnp.where(slot_group == g, ORDER[half * 4 + g], wanted)
        chosen = jnp.sum(jnp.where(slot_q == wanted, four, 0), axis=0, keepdims=True)
        pick = iota((LOCAL, LANES), 0) == chosen
        pick_send[half] = pick.astype(F32).astype(BF16)

    for f in range(FACES):
        lanes = pl.ds(f * LANES, LANES)
        wanted = link_v[f : f + 1, :]
        pick_local[:, lanes] = (iota((LOCAL, LANES), 0) == wanted).astype(F32).astype(BF16)
        for place, q in enumerate(ORDER):
            pick = iota((SLOTS, LANES), 0) + (LOCAL + q * SLOTS) == wanted
            pick_remote[pl.ds(place * SLOTS, SLOTS), lanes] = pick.astype(F32).astype(BF16)

    for place, origin in enumerate(origins):

        @pl.when(jnp.logical_not(inside(origin)))
        def _(place=place):
            for trade in range(2):
                incoming[trade, place] = jnp.zeros((PART, LANES), F32)

    sub = iota((8, LANES), 0)
    scale = jnp.where(sub % 4 == 0, 1.0, 3.0)
    coef = jnp.concatenate(
        [
            jnp.where(
                sub < 4,
                absorption_v[2 * pair : 2 * pair + 1, :],
                absorption_v[2 * pair + 1 : 2 * pair + 2, :],
            )
            * scale
            for pair in range(2)
        ],
        axis=1,
    )
    pen_sum_two = jnp.concatenate([pen_sum, pen_sum], axis=1)
    live_two = jnp.concatenate([live, live], axis=1)
    inv_denom = 1.0 / (coef + 0.5 * pen_sum_two)
    ratio = coef * inv_denom

    for pair in range(2):
        first = source_v[pl.ds(160 * pair, 80), :].reshape(10, 8, LANES)
        other = source_v[pl.ds(160 * pair + 80, 80), :].reshape(10, 8, LANES)
        even, odd = pair_up(first, other)
        lanes = pl.ds(pair * LANES, LANES)
        for p in range(10):
            rhs[2 * p, :, lanes] = even[p] * live
            rhs[2 * p + 1, :, lanes] = odd[p] * live

    def precondition(value, target):
        solved = times(mass_weights[...], value.reshape(FIELD, 2 * LANES))
        target[...] = solved.reshape(NODES, 8, 2 * LANES) * inv_denom[None]

    def fill_table(field):
        high, low = split(field[...])
        for h, part in enumerate((high, low)):
            for pair in range(2):
                block = jnp.concatenate(
                    [
                        jnp.concatenate(
                            [
                                part[FACE_NODE[t][f], :, pair * LANES : (pair + 1) * LANES]
                                for f in range(FACES)
                            ],
                            axis=1,
                        )
                        for t in range(TRI)
                    ],
                    axis=0,
                )
                table[pl.ds(h * ROWS + pair * 80, 80), :] = block.astype(BF16)

    group_of = iota((PART, LANES), 1) // SLOTS

    nearer = (at_z >= size_z // 2).astype(jnp.int32)

    def peer(half, g):
        reach = PEERS // 2 - g
        return jnp.where(half == 0, me - reach, me + reach), jnp.where(half == 0, me + reach, me - reach)

    def trade_copy(trade, half, g):
        place = half * 4 + g
        return remote(
            outgoing.at[trade, place],
            incoming.at[trade, place],
            send_sem.at[trade, place],
            recv_sem.at[trade, place],
            peer(half, g)[0],
        )

    def detour_copy(g):
        return remote(
            outgoing.at[0, g], held.at[g], send_sem.at[0, g], held_recv.at[g], me - column
        )

    def pass_copy(g):
        return remote(
            held.at[g],
            incoming.at[0, g],
            held_send.at[g],
            recv_sem.at[0, g],
            me + column - (REACH - g),
        )

    def pass_on():
        for g in range(REACH):

            @pl.when(passed < REACH - g)
            def _(g=g):
                detour_copy(g).wait_recv()
                pass_copy(g).start()

    def pass_done():
        for g in range(REACH):
            pl.when(passed < REACH - g)(pass_copy(g).wait_send)

    def send_traces(trade):
        for at, half in enumerate((nearer, 1 - nearer)):
            both = dot(table[...], pick_send[half])
            packed = both[:ROWS] + both[ROWS:]
            parts = [packed[j * PART : (j + 1) * PART] for j in range(4)]
            for g in range(4):
                message = None
                for j in range(4):
                    shift = (j - g) * SLOTS % LANES
                    part = pltpu.roll(parts[j], shift, 1) if shift else parts[j]
                    message = part if message is None else jnp.where(group_of == j, part, message)
                outgoing[trade, half * 4 + g] = message
            if trade == 0 and at == 0:
                pl.when(is_early)(await_partners)
                pl.when(is_passing)(pass_on)
            for g in range(4):
                wanted = inside(peer(half, g)[0])
                if trade == 0:
                    detour = jnp.logical_and(half == 0, detours(REACH - g))
                    pl.when(detour)(detour_copy(g).start)
                    wanted = jnp.logical_and(wanted, jnp.logical_not(detour))
                pl.when(wanted)(trade_copy(trade, half, g).start)

    def receive_traces(trade, near):
        for half in (nearer, 1 - nearer):
            for g in range(4):
                pl.when(inside(peer(half, g)[1]))(trade_copy(trade, half, g).wait_recv)
            blocks = []
            for j in range(4):
                gathered = None
                for g in range(4):
                    shift = (g - j) * SLOTS % LANES
                    part = incoming[trade, half * 4 + g]
                    part = pltpu.roll(part, shift, 1) if shift else part
                    gathered = part if gathered is None else jnp.where(group_of == g, part, gathered)
                blocks.append(gathered)
            high, low = split(jnp.concatenate(blocks, axis=0))
            received = jnp.concatenate([high, low], axis=0).astype(BF16)
            both = dot(received, pick_remote[pl.ds(pl.multiple_of(half * LANES, LANES), LANES), :])
            near = near + (both[:ROWS] + both[ROWS:])
        return near

    precondition(rhs[...], direction)
    fill_table(direction)
    send_traces(0)
    pl.when(is_early)(send_up)

    flux = jnp.zeros(square, F32)
    for d in range(3):
        ahead = thrice(stiffness_v[d])
        back = thrice(stiffness_v[d].T)
        from_flux = (row_of % 8) + (d + 1) == lane_of % 8
        from_flux = jnp.logical_and(from_flux, row_of % 4 == 0)
        to_flux = (lane_of % 8) + (d + 1) == row_of % 8
        to_flux = jnp.logical_and(to_flux, lane_of % 4 == 0)
        flux = jnp.where(from_flux, dot(dot(rows, ahead).astype(BF16), columns), flux)
        flux = jnp.where(to_flux, dot(dot(rows, back).astype(BF16), columns), flux)
    flux_weights[...] = flux.astype(BF16)

    geo_in = jnp.where(sub % 4 == 0, 1.0, 0.0)
    geo_out = geo_in
    for d in range(3):
        here = sub % 4 == d + 1
        geo_in = jnp.where(here, geometry_v[d : d + 1, :], geo_in)
        geo_out = jnp.where(here, -geometry_v[d : d + 1, :], geo_out)
    geo_in = jnp.concatenate([geo_in, geo_in], axis=1)
    geo_out = jnp.concatenate([geo_out, geo_out], axis=1)

    pen_node = []
    for node in range(NODES):
        value = None
        for t in range(TRI):
            for f in range(FACES):
                if FACE_NODE[t][f] == node:
                    value = pen[f] if value is None else value + pen[f]
        pen_node.append(jnp.concatenate([value, value], axis=1))
    pen_row = jnp.concatenate(pen, axis=1)
    orient_row = jnp.concatenate([orient_v[f : f + 1, :] for f in range(FACES)], axis=1)

    def apply_local(field):
        both = dot(table[...], pick_local[...])
        value = field[...]
        flux_term = times(flux_weights[...], (value * geo_in[None]).reshape(FIELD, 2 * LANES))
        return both[:ROWS] + both[ROWS:], flux_term.reshape(NODES, 8, 2 * LANES)

    def apply_remote(trade, field, solved, local, target):
        near, flux_term = local
        across = receive_traces(trade, near)
        total = [None] * NODES
        for t in range(TRI):
            sides = []
            for pair in range(2):
                def rows_of(node):
                    start = pair * 80 + node * 8
                    return across[start : start + 8]

                side = rows_of(TURNED[0][t])
                for o in range(1, 6):
                    if TURNED[o][t] != TURNED[0][t]:
                        side = jnp.where(orient_row == o, rows_of(TURNED[o][t]), side)
                sides.append(side * pen_row)
            for f in range(FACES):
                lanes = slice(f * LANES, (f + 1) * LANES)
                jump = jnp.concatenate([side[:, lanes] for side in sides], axis=1)
                node = FACE_NODE[t][f]
                total[node] = jump if total[node] is None else total[node] + jump
        for node in range(NODES):
            value = ratio * solved[node] + geo_out * flux_term[node]
            value = value + pen_node[node] * field[node] - total[node]
            target[node] = live_two * value

    across = [
        remote(level, along_in.at[k], along_send.at[k], along_recv.at[k], target)
        for k, target in enumerate(along_y)
    ]

    def down(chips):
        return [
            remote(top, top, down_send.at[i], down_recv.at[0], device(at_x, at_y, z, core))
            for i, z in enumerate(z for z in chips if z < size_z)
        ]

    def meet_column():
        column_in[mine] = own_best[...]
        rest = column_in.at[pl.ds(0, size_x * column - 1)]
        pltpu.make_async_copy(rest, rest, up_recv.at[0]).wait()
        level[...] = jnp.max(column_in[...], axis=0)
        for copy in across:
            copy.start()

    def meet_line():
        value = level[...]
        for k, copy in enumerate(across):
            copy.wait_recv()
            value = jnp.maximum(value, along_in[k])
        top[...] = value
        start_all(down(DOWN))

    def start_all(copies):
        for copy in copies:
            copy.start()

    def wait_all(copies):
        for copy in copies:
            copy.wait_send()

    def write_out(field, target):
        value = field[...]
        for pair in range(2):
            lanes = slice(pair * LANES, (pair + 1) * LANES)
            for p in range(10):
                even, odd = value[2 * p, :, lanes], value[2 * p + 1, :, lanes]
                low, high = pair_up(even[None], odd[None])
                target[pl.ds(160 * pair + 8 * p, 8), :] = low[0]
                target[pl.ds(160 * pair + 80 + 8 * p, 8), :] = high[0]

    local = apply_local(direction)
    pl.when(is_head)(meet_column)
    apply_remote(0, direction, rhs, local, applied)
    precondition(applied[...], second)
    fill_table(second)
    send_traces(1)
    local = apply_local(second)
    for field, target in (
        (direction, direction_out),
        (second, second_out),
        (rhs, rhs_out),
        (applied, applied_out),
    ):
        write_out(field, target)
    pl.when(is_head)(meet_line)
    apply_remote(1, second, applied, local, twice)
    write_out(twice, twice_out)
    for trade in range(2):
        for place, target in enumerate(targets):
            half, g = divmod(place, 4)
            pl.when(inside(target))(trade_copy(trade, half, g).wait_send)
    for wanted, copy in zip(up_to, up):
        pl.when(wanted)(copy.wait_send)
    pl.when(is_passing)(pass_done)
    pl.when(jnp.logical_not(is_head))(down(DOWN)[0].wait_recv)
    for z, chips in RELAY.items():
        pl.when(at_z == z)(functools.partial(start_all, down(chips)))

    inv_upper = 1.0 / jnp.max(top[...], axis=1, keepdims=True)
    first_weight = FIRST_WEIGHT * inv_upper
    second_weight = SECOND_WEIGHT * (inv_upper * inv_upper)
    weights_out[0:1, :] = jnp.broadcast_to(first_weight, (1, LANES))
    weights_out[1:2, :] = jnp.broadcast_to(second_weight, (1, LANES))

    pl.when(is_head)(functools.partial(wait_all, across + down(DOWN)))
    for z, chips in RELAY.items():
        pl.when(at_z == z)(functools.partial(wait_all, down(chips)))


def solution(mesh):
    n = mesh.shape["dom"]
    size_x, size_y, size_z = torus(n)
    along = max(size_y - 1, 1)

    def body(
        source, absorption, geometry, penalty, link, orient, send_index, live_count, mass, stiffness
    ):
        flat = source.transpose(0, 2, 1, 3).reshape(GASES * NODES * COMPS, LANES)
        operands = (
            flat,
            absorption,
            geometry,
            penalty,
            link,
            orient,
            send_index,
            live_count,
            mass,
            stiffness,
        )
        vmem = pltpu.VMEM
        field = vmem((NODES, 8, 2 * LANES), F32)
        dma = pltpu.SemaphoreType.DMA
        hbm = pl.BlockSpec(memory_space=pltpu.HBM)
        first, second, rhs, applied, twice, weights = pl.pallas_call(
            functools.partial(kernel, n),
            out_shape=[jax.ShapeDtypeStruct(flat.shape, F32)] * 5
            + [jax.ShapeDtypeStruct((2, LANES), F32)],
            in_specs=[hbm] * 3
            + [pl.BlockSpec(memory_space=vmem)]
            + [hbm] * 3
            + [pl.BlockSpec(memory_space=pltpu.SMEM)]
            + [hbm] * 2,
            out_specs=[pl.BlockSpec(memory_space=vmem)] * 6,
            scratch_shapes=[
                vmem((320, LANES), F32),
                vmem((4, LANES), F32),
                vmem((3, LANES), F32),
                vmem((4, LANES), jnp.int32),
                vmem((4, LANES), jnp.int32),
                vmem((1, PEERS, SLOTS), jnp.int32),
                vmem((NODES, NODES), F32),
                vmem((3, NODES, NODES), F32),
                field,
                field,
                field,
                field,
                field,
                vmem((FIELD, 3 * FIELD), BF16),
                vmem((FIELD, 3 * FIELD), BF16),
                vmem((2, LOCAL, LANES), BF16),
                vmem((LOCAL, LOCAL), BF16),
                vmem((REMOTE, LOCAL), BF16),
                vmem((2 * ROWS, LOCAL), BF16),
                vmem((2, PEERS, PART, LANES), F32),
                vmem((2, PEERS, PART, LANES), F32),
                vmem((REACH, PART, LANES), F32),
                vmem((1, LANES), F32),
                vmem((2 * size_z * size_x, 1, LANES), F32),
                vmem((along, 1, LANES), F32),
                vmem((1, LANES), F32),
                vmem((1, LANES), F32),
                dma((8,)),
                dma((2, PEERS)),
                dma((2, PEERS)),
                dma((REACH,)),
                dma((REACH,)),
                dma((2 * size_x,)),
                dma((1,)),
                dma((along,)),
                dma((along,)),
                dma((len(DOWN),)),
                dma((1,)),
            ],
            compiler_params=pltpu.CompilerParams(
                collective_id=0, has_side_effects=True, vmem_limit_bytes=32 * 2**20
            ),
            cost_estimate=pl.CostEstimate(
                flops=2_000_000_000, bytes_accessed=1_000_000, transcendentals=0
            ),
        )(*[
                value
                if value is live_count or value is penalty
                else pltpu.with_memory_space_constraint(value, pltpu.HBM)
                for value in operands
            ]
        )
        outs = (
            weights[0] * first + weights[1] * second,
            rhs - weights[0] * applied - weights[1] * twice,
        )
        return tuple(
            out.reshape(GASES, NODES, COMPS, LANES).transpose(0, 2, 1, 3) for out in outs
        )

    in_specs = (
        P(None, None, None, "dom"),
        P(None, "dom"),
        P(None, "dom"),
        P(None, "dom"),
        P(None, "dom"),
        P(None, "dom"),
        P("dom", None, None),
        P("dom"),
        P(),
        P(),
    )
    out_specs = (P(None, None, None, "dom"), P(None, None, None, "dom"))
    return jax.shard_map(body, mesh=mesh, in_specs=in_specs, out_specs=out_specs, check_vma=False)
```

```python
import functools

import jax
import jax.numpy as jnp
import numpy as np
from jax import lax
from jax.experimental import pallas as pl
from jax.experimental.pallas import tpu as pltpu
from jax.sharding import PartitionSpec as P

MESH = pl.DeviceIdType.MESH
F32 = jnp.float32
BF16 = jnp.bfloat16
GASES = 4
COMPS = 4
NODES = 20
FACES = 4
TRI = 10
SLOTS = 32
PEERS = 8
LANES = 128
OFFSETS = tuple(q + 1 if q < 4 else -(q - 3) for q in range(PEERS))
LOCAL = FACES * LANES
REMOTE = PEERS * SLOTS
ROWS = 2 * TRI * 8
PART = ROWS // 4
FIELD = NODES * 8


def node_tables():
    triangle = [(a, b, 3 - a - b) for a in range(4) for b in range(4 - a)]
    tetra_nodes = [
        (i, j, k, 3 - i - j - k) for i in range(4) for j in range(4 - i) for k in range(4 - i - j)
    ]
    face_index = np.zeros((10, 4), np.int32)
    for t in range(10):
        for f in range(4):
            coords = list(triangle[t])
            coords.insert(f, 0)
            face_index[t, f] = tetra_nodes.index(tuple(coords))
    orders = ((0, 1, 2), (1, 2, 0), (2, 0, 1), (0, 2, 1), (2, 1, 0), (1, 0, 2))
    turned = np.zeros((6, 10), np.int32)
    for o in range(6):
        for t in range(10):
            turned[o, t] = triangle.index(tuple((triangle[t][q] for q in orders[o])))
    return face_index.tolist(), turned.tolist()


FACE_NODE, TURNED = node_tables()


def step_weights():
    centre, half_width = (1.0 + 0.1) / 2.0, (1.0 - 0.1) / 2.0
    sigma_one = centre / half_width
    ratio = 1.0 / sigma_one
    ratio_new = 1.0 / (2.0 * sigma_one - ratio)
    step = 2.0 * ratio_new / half_width
    return (1.0 + ratio_new * ratio) / centre + step, -step / centre


FIRST_WEIGHT, SECOND_WEIGHT = step_weights()


ORDER = (7, 6, 5, 4, 3, 2, 1, 0)
DOWN = (4, 1, 5, 2, 3, 8, 12, 9, 10, 11)
RELAY = {4: (6, 7), 12: (13, 14, 15)}
LOOKOUT = (4, 1, 2)
REACH = 4
EARLY = 4


def torus(count):
    chips = count // 2
    z = 16 if chips >= 256 else min(chips, 4)
    y = min(4, chips // z)
    return chips // (z * y), y, z


def iota(shape, axis):
    return lax.broadcasted_iota(jnp.int32, shape, axis)


def split(value):
    high = value.astype(BF16).astype(F32)
    return high, value - high


def dot(a, b):
    return jnp.dot(a, b, preferred_element_type=F32)


def invert(matrix):
    size = matrix.shape[0]
    lane, sub = iota((size, LANES), 1), iota((size, LANES), 0)
    planes = [jnp.broadcast_to(matrix[:, i : i + 1], (size, LANES)) for i in range(size)]
    state = jnp.stack(planes, axis=0)
    for k in range(size):
        pivot = 1.0 / state[k, k : k + 1]
        row = state[k] * pivot
        change = jnp.where(sub == k, 1.0 + pivot, row)
        row = jnp.where(sub == k, pivot, row)
        rest = state - state[:, k : k + 1, :] * change[None]
        state = jnp.concatenate(
            [part for part in (rest[:k], row[None], rest[k + 1 :]) if part.shape[0]], axis=0
        )
    inverse = state[0]
    for i in range(1, size):
        inverse = jnp.where(lane == i, state[i], inverse)
    return inverse[:, :size]


def spread_rows():
    return (iota((FIELD, NODES), 0) // 8 == iota((FIELD, NODES), 1)).astype(F32).astype(BF16)


def spread_columns():
    shape = (3 * NODES, 3 * FIELD)
    return (iota(shape, 1) // 8 == iota(shape, 0)).astype(F32).astype(BF16)


def thrice(matrix):
    high, low = split(matrix)
    return jnp.concatenate([high, high, low], axis=1).astype(BF16)


def times(weights, field):
    high, low = split(field)
    return dot(weights, jnp.concatenate([high, low, high], axis=0).astype(BF16))


def pair_up(first, second):
    sub = iota(first.shape, 1)
    even = jnp.where(sub < 4, first, pltpu.roll(second, 4, 1))
    odd = jnp.where(sub < 4, pltpu.roll(first, 4, 1), second)
    return even, odd


def kernel(
    n,
    source,
    absorption,
    geometry,
    penalty_v,
    link,
    orient,
    send_index,
    live_count,
    mass,
    stiffness,
    direction_out,
    second_out,
    rhs_out,
    applied_out,
    twice_out,
    weights_out,
    source_v,
    absorption_v,
    geometry_v,
    link_v,
    orient_v,
    send_v,
    mass_v,
    stiffness_v,
    rhs,
    direction,
    applied,
    second,
    twice,
    mass_weights,
    flux_weights,
    pick_send,
    pick_local,
    pick_remote,
    table,
    outgoing,
    incoming,
    held,
    own_best,
    column_in,
    along_in,
    look_in,
    level,
    top,
    in_sem,
    send_sem,
    recv_sem,
    held_send,
    held_recv,
    up_send,
    up_recv,
    along_send,
    along_recv,
    look_send,
    look_recv,
    down_send,
    down_recv,
):
    me = lax.axis_index("dom")
    size_x, size_y, size_z = torus(n)
    core = lax.rem(me, 2)
    at_z = lax.rem(me // 2, size_z)
    at_y = lax.rem(me // (2 * size_z), size_y)
    at_x = me // (2 * size_z * size_y)

    def device(x, y, z, c):
        return ((x * size_y + y) * size_z + z) * 2 + c

    def inside(index):
        return jnp.logical_and(index >= 0, index < n)

    targets = [me + OFFSETS[q] for q in ORDER]
    origins = [me - OFFSETS[q] for q in ORDER]
    other_y = [k + (k >= at_y).astype(jnp.int32) for k in range(size_y - 1)]
    along_x = [device(lax.rem(at_x + k, size_x), at_y, at_z, core) for k in range(1, size_x)]
    along_y = [device(at_x, y, at_z, core) for y in other_y]
    lookouts = [z for z in LOOKOUT if z < size_z]
    is_head = at_z == 0
    is_lookout = jnp.logical_and(
        at_y == 0, functools.reduce(jnp.logical_or, [at_z == z for z in lookouts])
    )
    is_early = at_z < EARLY

    column = 2 * size_z
    plane = column * size_y
    across_planes = size_x > 1 and size_z >= 4
    in_plane = lax.rem(me, plane)
    passed = in_plane - (plane - column)
    is_passing = jnp.logical_and(
        jnp.logical_and(passed >= 0, passed < REACH), jnp.logical_and(me + column < n, across_planes)
    )
    is_detoured = jnp.logical_and(
        in_plane < REACH, jnp.logical_and(me >= plane, across_planes)
    )

    def detours(reach):
        return jnp.logical_and(is_detoured, in_plane < reach)

    barrier = pltpu.get_barrier_semaphore()

    def greet(target):
        pl.semaphore_signal(barrier, inc=1, device_id=(target,), device_id_type=MESH)

    loads = []
    for i, (src, dst) in enumerate(
        (
            (mass, mass_v),
            (send_index, send_v),
            (source, source_v),
            (absorption, absorption_v),
            (geometry, geometry_v),
            (link, link_v),
            (orient, orient_v),
            (stiffness, stiffness_v),
        )
    ):
        loads.append(pltpu.make_async_copy(src, dst, in_sem.at[i]))
    loads[0].start()
    for reach in range(REACH, 0, -1):
        pl.when(inside(me - reach))(functools.partial(greet, me - reach))
        ahead = me + reach
        over = jnp.logical_and(in_plane + reach >= plane, across_planes)
        pl.when(inside(ahead))(functools.partial(greet, jnp.where(over, ahead - column, ahead)))
    pl.when(is_passing)(functools.partial(greet, me + column))

    for copy in loads[1:]:
        copy.start()
    @pl.when(is_lookout)
    def _():
        for y in range(1, size_y):
            greet(device(at_x, y, 0, core))

    @pl.when(is_head)
    def _():
        for z in sorted(range(1, size_z), key=lambda z: abs(z - size_z // 2 - 1)):
            for x in range(size_x):
                for c in range(2):
                    greet(device(x, at_y, z, c))
        greet(device(at_x, at_y, at_z, 1 - core))
        for target in along_x:
            for c in range(2):
                greet(target - core + c)
        for target in along_y:
            greet(target)

    live = (iota((1, LANES), 1) < live_count[0]).astype(F32)
    pen = [penalty_v[f : f + 1, :] for f in range(FACES)]
    pen_sum = pen[0] + pen[1] + pen[2] + pen[3]
    best = jnp.where(live > 0.5, 1.0 + 0.25 * pen_sum, 0.0)
    own_best[...] = best

    def remote(src, dst, send, recv, target):
        return pltpu.make_async_remote_copy(
            src_ref=src,
            dst_ref=dst,
            send_sem=send,
            recv_sem=recv,
            device_id=(target,),
            device_id_type=MESH,
        )

    mine = at_x * column + at_z * 2 + core
    up, up_to = [], []
    for x in range(size_x):
        for c in range(2):
            target = device(x, at_y, 0, c)
            up.append(
                remote(own_best, column_in.at[mine], up_send.at[len(up)], up_recv.at[0], target)
            )
            up_to.append(target != me)

    def count(wanted):
        return sum([each.astype(jnp.int32) for each in wanted])

    partners = count(up_to) + is_head.astype(jnp.int32) * len(along_y)
    partners = partners + count([inside(me + reach) for reach in range(1, REACH + 1)])
    partners = partners + count(
        [
            jnp.logical_and(inside(me - reach), jnp.logical_not(detours(reach)))
            for reach in range(1, REACH + 1)
        ]
    )
    partners = partners + is_detoured.astype(jnp.int32)
    partners = partners + jnp.logical_and(is_head, at_y > 0).astype(jnp.int32) * len(lookouts)
    partners = partners + is_passing.astype(jnp.int32) * (REACH - passed)

    def await_partners():
        pl.semaphore_wait(barrier, partners)

    def send_up():
        for wanted, copy in zip(up_to, up):
            pl.when(wanted)(copy.start)

    @pl.when(jnp.logical_not(is_early))
    def _():
        await_partners()
        send_up()

    for copy in loads:
        copy.wait()

    rows = spread_rows()
    columns = spread_columns()
    inverse = thrice(invert(mass_v[...]))
    square = (FIELD, 3 * FIELD)
    lane_of, row_of = iota(square, 1), iota(square, 0)
    wide = dot(dot(rows, inverse).astype(BF16), columns)
    mass_weights[...] = jnp.where(lane_of % 8 == row_of % 8, wide, 0.0).astype(BF16)

    sends = send_v[0]
    four = jnp.concatenate([sends, sends, sends, sends], axis=1)
    slot_q, slot_group = iota((PEERS, LANES), 0), iota((PEERS, LANES), 1) // SLOTS
    for half in range(2):
        wanted = jnp.zeros((PEERS, LANES), jnp.int32)
        for g in range(4):
            wanted = jnp.where(slot_group == g, ORDER[half * 4 + g], wanted)
        chosen = jnp.sum(jnp.where(slot_q == wanted, four, 0), axis=0, keepdims=True)
        pick = iota((LOCAL, LANES), 0) == chosen
        pick_send[half] = pick.astype(F32).astype(BF16)

    for f in range(FACES):
        lanes = pl.ds(f * LANES, LANES)
        wanted = link_v[f : f + 1, :]
        pick_local[:, lanes] = (iota((LOCAL, LANES), 0) == wanted).astype(F32).astype(BF16)
        for place, q in enumerate(ORDER):
            pick = iota((SLOTS, LANES), 0) + (LOCAL + q * SLOTS) == wanted
            pick_remote[pl.ds(place * SLOTS, SLOTS), lanes] = pick.astype(F32).astype(BF16)

    for place, origin in enumerate(origins):

        @pl.when(jnp.logical_not(inside(origin)))
        def _(place=place):
            for trade in range(2):
                incoming[trade, place] = jnp.zeros((PART, LANES), F32)

    sub = iota((8, LANES), 0)
    scale = jnp.where(sub % 4 == 0, 1.0, 3.0)
    coef = jnp.concatenate(
        [
            jnp.where(
                sub < 4,
                absorption_v[2 * pair : 2 * pair + 1, :],
                absorption_v[2 * pair + 1 : 2 * pair + 2, :],
            )
            * scale
            for pair in range(2)
        ],
        axis=1,
    )
    pen_sum_two = jnp.concatenate([pen_sum, pen_sum], axis=1)
    live_two = jnp.concatenate([live, live], axis=1)
    inv_denom = 1.0 / (coef + 0.5 * pen_sum_two)
    ratio = coef * inv_denom

    for pair in range(2):
        first = source_v[pl.ds(160 * pair, 80), :].reshape(10, 8, LANES)
        other = source_v[pl.ds(160 * pair + 80, 80), :].reshape(10, 8, LANES)
        even, odd = pair_up(first, other)
        lanes = pl.ds(pair * LANES, LANES)
        for p in range(10):
            rhs[2 * p, :, lanes] = even[p] * live
            rhs[2 * p + 1, :, lanes] = odd[p] * live

    def precondition(value, target):
        solved = times(mass_weights[...], value.reshape(FIELD, 2 * LANES))
        target[...] = solved.reshape(NODES, 8, 2 * LANES) * inv_denom[None]

    def fill_table(field):
        high, low = split(field[...])
        for h, part in enumerate((high, low)):
            for pair in range(2):
                block = jnp.concatenate(
                    [
                        jnp.concatenate(
                            [
                                part[FACE_NODE[t][f], :, pair * LANES : (pair + 1) * LANES]
                                for f in range(FACES)
                            ],
                            axis=1,
                        )
                        for t in range(TRI)
                    ],
                    axis=0,
                )
                table[pl.ds(h * ROWS + pair * 80, 80), :] = block.astype(BF16)

    group_of = iota((PART, LANES), 1) // SLOTS

    nearer = (at_z >= size_z // 2).astype(jnp.int32)

    def peer(half, g):
        reach = PEERS // 2 - g
        return jnp.where(half == 0, me - reach, me + reach), jnp.where(half == 0, me + reach, me - reach)

    def trade_copy(trade, half, g):
        place = half * 4 + g
        return remote(
            outgoing.at[trade, place],
            incoming.at[trade, place],
            send_sem.at[trade, place],
            recv_sem.at[trade, place],
            peer(half, g)[0],
        )

    def detour_copy(g):
        return remote(
            outgoing.at[0, g], held.at[g], send_sem.at[0, g], held_recv.at[g], me - column
        )

    def pass_copy(g):
        return remote(
            held.at[g],
            incoming.at[0, g],
            held_send.at[g],
            recv_sem.at[0, g],
            me + column - (REACH - g),
        )

    def pass_on():
        for g in range(REACH):

            @pl.when(passed < REACH - g)
            def _(g=g):
                detour_copy(g).wait_recv()
                pass_copy(g).start()

    def pass_done():
        for g in range(REACH):
            pl.when(passed < REACH - g)(pass_copy(g).wait_send)

    def send_traces(trade):
        for at, half in enumerate((nearer, 1 - nearer)):
            both = dot(table[...], pick_send[half])
            packed = both[:ROWS] + both[ROWS:]
            parts = [packed[j * PART : (j + 1) * PART] for j in range(4)]
            for g in range(4):
                message = None
                for j in range(4):
                    shift = (j - g) * SLOTS % LANES
                    part = pltpu.roll(parts[j], shift, 1) if shift else parts[j]
                    message = part if message is None else jnp.where(group_of == j, part, message)
                outgoing[trade, half * 4 + g] = message
            if trade == 0 and at == 0:
                pl.when(is_early)(await_partners)
                pl.when(is_passing)(pass_on)
            for g in range(4):
                wanted = inside(peer(half, g)[0])
                if trade == 0:
                    detour = jnp.logical_and(half == 0, detours(REACH - g))
                    pl.when(detour)(detour_copy(g).start)
                    wanted = jnp.logical_and(wanted, jnp.logical_not(detour))
                pl.when(wanted)(trade_copy(trade, half, g).start)

    def receive_traces(trade, near):
        for half in (nearer, 1 - nearer):
            for g in range(4):
                pl.when(inside(peer(half, g)[1]))(trade_copy(trade, half, g).wait_recv)
            blocks = []
            for j in range(4):
                gathered = None
                for g in range(4):
                    shift = (g - j) * SLOTS % LANES
                    part = incoming[trade, half * 4 + g]
                    part = pltpu.roll(part, shift, 1) if shift else part
                    gathered = part if gathered is None else jnp.where(group_of == g, part, gathered)
                blocks.append(gathered)
            high, low = split(jnp.concatenate(blocks, axis=0))
            received = jnp.concatenate([high, low], axis=0).astype(BF16)
            both = dot(received, pick_remote[pl.ds(pl.multiple_of(half * LANES, LANES), LANES), :])
            near = near + (both[:ROWS] + both[ROWS:])
        return near

    precondition(rhs[...], direction)
    fill_table(direction)
    send_traces(0)
    pl.when(is_early)(send_up)

    flux = jnp.zeros(square, F32)
    for d in range(3):
        ahead = thrice(stiffness_v[d])
        back = thrice(stiffness_v[d].T)
        from_flux = (row_of % 8) + (d + 1) == lane_of % 8
        from_flux = jnp.logical_and(from_flux, row_of % 4 == 0)
        to_flux = (lane_of % 8) + (d + 1) == row_of % 8
        to_flux = jnp.logical_and(to_flux, lane_of % 4 == 0)
        flux = jnp.where(from_flux, dot(dot(rows, ahead).astype(BF16), columns), flux)
        flux = jnp.where(to_flux, dot(dot(rows, back).astype(BF16), columns), flux)
    flux_weights[...] = flux.astype(BF16)

    geo_in = jnp.where(sub % 4 == 0, 1.0, 0.0)
    geo_out = geo_in
    for d in range(3):
        here = sub % 4 == d + 1
        geo_in = jnp.where(here, geometry_v[d : d + 1, :], geo_in)
        geo_out = jnp.where(here, -geometry_v[d : d + 1, :], geo_out)
    geo_in = jnp.concatenate([geo_in, geo_in], axis=1)
    geo_out = jnp.concatenate([geo_out, geo_out], axis=1)

    pen_node = []
    for node in range(NODES):
        value = None
        for t in range(TRI):
            for f in range(FACES):
                if FACE_NODE[t][f] == node:
                    value = pen[f] if value is None else value + pen[f]
        pen_node.append(jnp.concatenate([value, value], axis=1))
    pen_row = jnp.concatenate(pen, axis=1)
    orient_row = jnp.concatenate([orient_v[f : f + 1, :] for f in range(FACES)], axis=1)

    def apply_local(field):
        both = dot(table[...], pick_local[...])
        value = field[...]
        flux_term = times(flux_weights[...], (value * geo_in[None]).reshape(FIELD, 2 * LANES))
        return both[:ROWS] + both[ROWS:], flux_term.reshape(NODES, 8, 2 * LANES)

    def apply_remote(trade, field, solved, local, target):
        near, flux_term = local
        across = receive_traces(trade, near)
        total = [None] * NODES
        for t in range(TRI):
            sides = []
            for pair in range(2):
                def rows_of(node):
                    start = pair * 80 + node * 8
                    return across[start : start + 8]

                side = rows_of(TURNED[0][t])
                for o in range(1, 6):
                    if TURNED[o][t] != TURNED[0][t]:
                        side = jnp.where(orient_row == o, rows_of(TURNED[o][t]), side)
                sides.append(side * pen_row)
            for f in range(FACES):
                lanes = slice(f * LANES, (f + 1) * LANES)
                jump = jnp.concatenate([side[:, lanes] for side in sides], axis=1)
                node = FACE_NODE[t][f]
                total[node] = jump if total[node] is None else total[node] + jump
        for node in range(NODES):
            value = ratio * solved[node] + geo_out * flux_term[node]
            value = value + pen_node[node] * field[node] - total[node]
            target[node] = live_two * value

    across = []
    for k, y in enumerate(other_y):
        slot = at_y - (at_y > y).astype(jnp.int32)
        target = device(at_x, y, at_z, core)
        across.append(
            remote(level, along_in.at[slot], along_send.at[k], along_recv.at[slot], target)
        )
    ahead_of = [
        remote(
            level, look_in.at[at_y], look_send.at[i], look_recv.at[at_y], device(at_x, 0, z, core)
        )
        for i, z in enumerate(lookouts)
    ]

    def look_out():
        value = None
        for y in range(size_y):
            remote(level, look_in.at[y], look_send.at[0], look_recv.at[y], me + 1 - 2 * core).wait_recv()
            value = look_in[y] if value is None else jnp.maximum(value, look_in[y])
        top[...] = value

    def down(chips):
        return [
            remote(top, top, down_send.at[i], down_recv.at[0], device(at_x, at_y, z, core))
            for i, z in enumerate(z for z in chips if z < size_z)
        ]

    down_to = [
        jnp.logical_or(at_y > 0, z not in lookouts) for z in DOWN if z < size_z
    ]

    def heads_done():
        wait_all(across + ahead_of)
        for wanted, copy in zip(down_to, down(DOWN)):
            pl.when(wanted)(copy.wait_send)

    def meet_column():
        column_in[mine] = own_best[...]
        rest = column_in.at[pl.ds(0, size_x * column - 1)]
        pltpu.make_async_copy(rest, rest, up_recv.at[0]).wait()
        chains = column_in[...].reshape(8, size_x * column // 8, 1, LANES)
        level[...] = jnp.max(jnp.max(chains, axis=0), axis=0)
        if across:
            pl.when(at_y > 0)(across[0].start)
        start_all(ahead_of)
        if across:
            pl.when(at_y == 0)(across[0].start)
        start_all(across[1:])

    def meet_line():
        value = level[...]
        for k in range(size_y - 1):
            remote(level, along_in.at[k], along_send.at[k], along_recv.at[k], me + 1 - 2 * core).wait_recv()
            value = jnp.maximum(value, along_in[k])
        top[...] = value
        for wanted, copy in zip(down_to, down(DOWN)):
            pl.when(wanted)(copy.start)

    def start_all(copies):
        for copy in copies:
            copy.start()

    def wait_all(copies):
        for copy in copies:
            copy.wait_send()

    def write_out(field, target):
        value = field[...]
        for pair in range(2):
            lanes = slice(pair * LANES, (pair + 1) * LANES)
            for p in range(10):
                even, odd = value[2 * p, :, lanes], value[2 * p + 1, :, lanes]
                low, high = pair_up(even[None], odd[None])
                target[pl.ds(160 * pair + 8 * p, 8), :] = low[0]
                target[pl.ds(160 * pair + 80 + 8 * p, 8), :] = high[0]

    local = apply_local(direction)
    pl.when(is_head)(meet_column)
    apply_remote(0, direction, rhs, local, applied)
    precondition(applied[...], second)
    fill_table(second)
    send_traces(1)
    local = apply_local(second)
    for field, target in (
        (direction, direction_out),
        (second, second_out),
        (rhs, rhs_out),
        (applied, applied_out),
    ):
        write_out(field, target)
    pl.when(is_head)(meet_line)
    apply_remote(1, second, applied, local, twice)
    write_out(twice, twice_out)
    for trade in range(2):
        for place, target in enumerate(targets):
            half, g = divmod(place, 4)
            pl.when(inside(target))(trade_copy(trade, half, g).wait_send)
    for wanted, copy in zip(up_to, up):
        pl.when(wanted)(copy.wait_send)
    pl.when(is_passing)(pass_done)
    pl.when(is_lookout)(look_out)
    pl.when(jnp.logical_not(jnp.logical_or(is_head, is_lookout)))(down(DOWN)[0].wait_recv)
    for z, chips in RELAY.items():
        pl.when(at_z == z)(functools.partial(start_all, down(chips)))

    inv_upper = 1.0 / jnp.max(top[...], axis=1, keepdims=True)
    first_weight = FIRST_WEIGHT * inv_upper
    second_weight = SECOND_WEIGHT * (inv_upper * inv_upper)
    weights_out[0:1, :] = jnp.broadcast_to(first_weight, (1, LANES))
    weights_out[1:2, :] = jnp.broadcast_to(second_weight, (1, LANES))

    pl.when(is_head)(heads_done)
    for z, chips in RELAY.items():
        pl.when(at_z == z)(functools.partial(wait_all, down(chips)))


def solution(mesh):
    n = mesh.shape["dom"]
    size_x, size_y, size_z = torus(n)
    along = max(size_y - 1, 1)

    def body(
        source, absorption, geometry, penalty, link, orient, send_index, live_count, mass, stiffness
    ):
        flat = source.transpose(0, 2, 1, 3).reshape(GASES * NODES * COMPS, LANES)
        operands = (
            flat,
            absorption,
            geometry,
            penalty,
            link,
            orient,
            send_index,
            live_count,
            mass,
            stiffness,
        )
        vmem = pltpu.VMEM
        field = vmem((NODES, 8, 2 * LANES), F32)
        dma = pltpu.SemaphoreType.DMA
        hbm = pl.BlockSpec(memory_space=pltpu.HBM)
        first, second, rhs, applied, twice, weights = pl.pallas_call(
            functools.partial(kernel, n),
            out_shape=[jax.ShapeDtypeStruct(flat.shape, F32)] * 5
            + [jax.ShapeDtypeStruct((2, LANES), F32)],
            in_specs=[hbm] * 3
            + [pl.BlockSpec(memory_space=vmem)]
            + [hbm] * 3
            + [pl.BlockSpec(memory_space=pltpu.SMEM)]
            + [hbm] * 2,
            out_specs=[pl.BlockSpec(memory_space=vmem)] * 6,
            scratch_shapes=[
                vmem((320, LANES), F32),
                vmem((4, LANES), F32),
                vmem((3, LANES), F32),
                vmem((4, LANES), jnp.int32),
                vmem((4, LANES), jnp.int32),
                vmem((1, PEERS, SLOTS), jnp.int32),
                vmem((NODES, NODES), F32),
                vmem((3, NODES, NODES), F32),
                field,
                field,
                field,
                field,
                field,
                vmem((FIELD, 3 * FIELD), BF16),
                vmem((FIELD, 3 * FIELD), BF16),
                vmem((2, LOCAL, LANES), BF16),
                vmem((LOCAL, LOCAL), BF16),
                vmem((REMOTE, LOCAL), BF16),
                vmem((2 * ROWS, LOCAL), BF16),
                vmem((2, PEERS, PART, LANES), F32),
                vmem((2, PEERS, PART, LANES), F32),
                vmem((REACH, PART, LANES), F32),
                vmem((1, LANES), F32),
                vmem((2 * size_z * size_x, 1, LANES), F32),
                vmem((along, 1, LANES), F32),
                vmem((size_y, 1, LANES), F32),
                vmem((1, LANES), F32),
                vmem((1, LANES), F32),
                dma((8,)),
                dma((2, PEERS)),
                dma((2, PEERS)),
                dma((REACH,)),
                dma((REACH,)),
                dma((2 * size_x,)),
                dma((1,)),
                dma((along,)),
                dma((along,)),
                dma((len(LOOKOUT),)),
                dma((size_y,)),
                dma((len(DOWN),)),
                dma((1,)),
            ],
            compiler_params=pltpu.CompilerParams(
                collective_id=0, has_side_effects=True, vmem_limit_bytes=32 * 2**20
            ),
            cost_estimate=pl.CostEstimate(
                flops=2_000_000_000, bytes_accessed=1_000_000, transcendentals=0
            ),
        )(*[
                value
                if value is live_count or value is penalty
                else pltpu.with_memory_space_constraint(value, pltpu.HBM)
                for value in operands
            ]
        )
        outs = (
            weights[0] * first + weights[1] * second,
            rhs - weights[0] * applied - weights[1] * twice,
        )
        return tuple(
            out.reshape(GASES, NODES, COMPS, LANES).transpose(0, 2, 1, 3) for out in outs
        )

    in_specs = (
        P(None, None, None, "dom"),
        P(None, "dom"),
        P(None, "dom"),
        P(None, "dom"),
        P(None, "dom"),
        P(None, "dom"),
        P("dom", None, None),
        P("dom"),
        P(),
        P(),
    )
    out_specs = (P(None, None, None, "dom"), P(None, None, None, "dom"))
    return jax.shard_map(body, mesh=mesh, in_specs=in_specs, out_specs=out_specs, check_vma=False)
```

```python
import functools

import jax
import jax.numpy as jnp
import numpy as np
from jax import lax
from jax.experimental import pallas as pl
from jax.experimental.pallas import tpu as pltpu
from jax.sharding import PartitionSpec as P

MESH = pl.DeviceIdType.MESH
F32 = jnp.float32
BF16 = jnp.bfloat16
GASES = 4
COMPS = 4
NODES = 20
FACES = 4
TRI = 10
SLOTS = 32
PEERS = 8
LANES = 128
OFFSETS = tuple(q + 1 if q < 4 else -(q - 3) for q in range(PEERS))
LOCAL = FACES * LANES
REMOTE = PEERS * SLOTS
ROWS = 2 * TRI * 8
PART = ROWS // 4
FIELD = NODES * 8


def node_tables():
    triangle = [(a, b, 3 - a - b) for a in range(4) for b in range(4 - a)]
    tetra_nodes = [
        (i, j, k, 3 - i - j - k) for i in range(4) for j in range(4 - i) for k in range(4 - i - j)
    ]
    face_index = np.zeros((10, 4), np.int32)
    for t in range(10):
        for f in range(4):
            coords = list(triangle[t])
            coords.insert(f, 0)
            face_index[t, f] = tetra_nodes.index(tuple(coords))
    orders = ((0, 1, 2), (1, 2, 0), (2, 0, 1), (0, 2, 1), (2, 1, 0), (1, 0, 2))
    turned = np.zeros((6, 10), np.int32)
    for o in range(6):
        for t in range(10):
            turned[o, t] = triangle.index(tuple((triangle[t][q] for q in orders[o])))
    return face_index.tolist(), turned.tolist()


FACE_NODE, TURNED = node_tables()


def step_weights():
    centre, half_width = (1.0 + 0.1) / 2.0, (1.0 - 0.1) / 2.0
    sigma_one = centre / half_width
    ratio = 1.0 / sigma_one
    ratio_new = 1.0 / (2.0 * sigma_one - ratio)
    step = 2.0 * ratio_new / half_width
    return (1.0 + ratio_new * ratio) / centre + step, -step / centre


FIRST_WEIGHT, SECOND_WEIGHT = step_weights()


ORDER = (7, 6, 5, 4, 3, 2, 1, 0)
DOWN = (4, 1, 2, 3, 5, 8, 12, 9, 10, 11)
RELAY = {4: (6, 7), 12: (13, 14, 15)}
LOOKOUT = (4, 1, 2)
REACH = 4
EARLY = 4


def torus(count):
    chips = count // 2
    z = 16 if chips >= 256 else min(chips, 4)
    y = min(4, chips // z)
    return chips // (z * y), y, z


def iota(shape, axis):
    return lax.broadcasted_iota(jnp.int32, shape, axis)


def split(value):
    high = value.astype(BF16).astype(F32)
    return high, value - high


def dot(a, b):
    return jnp.dot(a, b, preferred_element_type=F32)


def invert(matrix):
    size = matrix.shape[0]
    lane, sub = iota((size, LANES), 1), iota((size, LANES), 0)
    planes = [jnp.broadcast_to(matrix[:, i : i + 1], (size, LANES)) for i in range(size)]
    state = jnp.stack(planes, axis=0)
    for k in range(size):
        pivot = 1.0 / state[k, k : k + 1]
        row = state[k] * pivot
        change = jnp.where(sub == k, 1.0 + pivot, row)
        row = jnp.where(sub == k, pivot, row)
        rest = state - state[:, k : k + 1, :] * change[None]
        state = jnp.concatenate(
            [part for part in (rest[:k], row[None], rest[k + 1 :]) if part.shape[0]], axis=0
        )
    inverse = state[0]
    for i in range(1, size):
        inverse = jnp.where(lane == i, state[i], inverse)
    return inverse[:, :size]


def spread_rows():
    return (iota((FIELD, NODES), 0) // 8 == iota((FIELD, NODES), 1)).astype(F32).astype(BF16)


def spread_columns():
    shape = (3 * NODES, 3 * FIELD)
    return (iota(shape, 1) // 8 == iota(shape, 0)).astype(F32).astype(BF16)


def thrice(matrix):
    high, low = split(matrix)
    return jnp.concatenate([high, high, low], axis=1).astype(BF16)


def times(weights, field):
    high, low = split(field)
    return dot(weights, jnp.concatenate([high, low, high], axis=0).astype(BF16))


def pair_up(first, second):
    sub = iota(first.shape, 1)
    even = jnp.where(sub < 4, first, pltpu.roll(second, 4, 1))
    odd = jnp.where(sub < 4, pltpu.roll(first, 4, 1), second)
    return even, odd


def kernel(
    n,
    source,
    absorption,
    geometry,
    penalty_v,
    link,
    orient,
    send_index,
    live_count,
    mass,
    stiffness,
    direction_out,
    second_out,
    rhs_out,
    applied_out,
    twice_out,
    weights_out,
    source_v,
    absorption_v,
    geometry_v,
    link_v,
    orient_v,
    send_v,
    mass_v,
    stiffness_v,
    rhs,
    direction,
    applied,
    second,
    twice,
    mass_weights,
    flux_weights,
    pick_send,
    pick_local,
    pick_remote,
    table,
    outgoing,
    incoming,
    held,
    own_best,
    column_in,
    along_in,
    look_in,
    level,
    top,
    in_sem,
    send_sem,
    recv_sem,
    held_send,
    held_recv,
    up_send,
    up_recv,
    along_send,
    along_recv,
    look_send,
    look_recv,
    down_send,
    down_recv,
):
    me = lax.axis_index("dom")
    size_x, size_y, size_z = torus(n)
    core = lax.rem(me, 2)
    at_z = lax.rem(me // 2, size_z)
    at_y = lax.rem(me // (2 * size_z), size_y)
    at_x = me // (2 * size_z * size_y)

    def device(x, y, z, c):
        return ((x * size_y + y) * size_z + z) * 2 + c

    def inside(index):
        return jnp.logical_and(index >= 0, index < n)

    targets = [me + OFFSETS[q] for q in ORDER]
    origins = [me - OFFSETS[q] for q in ORDER]
    other_y = [k + (k >= at_y).astype(jnp.int32) for k in range(size_y - 1)]
    along_x = [device(lax.rem(at_x + k, size_x), at_y, at_z, core) for k in range(1, size_x)]
    along_y = [device(at_x, y, at_z, core) for y in other_y]
    lookouts = [z for z in LOOKOUT if z < size_z]
    is_head = at_z == 0
    is_lookout = jnp.logical_and(
        at_y == 0, functools.reduce(jnp.logical_or, [at_z == z for z in lookouts])
    )
    is_early = at_z < EARLY

    column = 2 * size_z
    plane = column * size_y
    across_planes = size_x > 1 and size_z >= 4
    in_plane = lax.rem(me, plane)
    passed = in_plane - (plane - column)
    is_passing = jnp.logical_and(
        jnp.logical_and(passed >= 0, passed < REACH), jnp.logical_and(me + column < n, across_planes)
    )
    is_detoured = jnp.logical_and(
        in_plane < REACH, jnp.logical_and(me >= plane, across_planes)
    )

    def detours(reach):
        return jnp.logical_and(is_detoured, in_plane < reach)

    barrier = pltpu.get_barrier_semaphore()

    def greet(target):
        pl.semaphore_signal(barrier, inc=1, device_id=(target,), device_id_type=MESH)

    loads = []
    for i, (src, dst) in enumerate(
        (
            (mass, mass_v),
            (send_index, send_v),
            (source, source_v),
            (absorption, absorption_v),
            (geometry, geometry_v),
            (link, link_v),
            (orient, orient_v),
            (stiffness, stiffness_v),
        )
    ):
        loads.append(pltpu.make_async_copy(src, dst, in_sem.at[i]))
    loads[0].start()
    for reach in range(REACH, 0, -1):
        pl.when(inside(me - reach))(functools.partial(greet, me - reach))
        ahead = me + reach
        over = jnp.logical_and(in_plane + reach >= plane, across_planes)
        pl.when(inside(ahead))(functools.partial(greet, jnp.where(over, ahead - column, ahead)))
    pl.when(is_passing)(functools.partial(greet, me + column))

    for copy in loads[1:]:
        copy.start()
    @pl.when(is_lookout)
    def _():
        for y in range(1, size_y):
            greet(device(at_x, y, 0, core))

    @pl.when(is_head)
    def _():
        for z in sorted(range(1, size_z), key=lambda z: abs(z - size_z // 2 - 1)):
            for x in range(size_x):
                for c in range(2):
                    greet(device(x, at_y, z, c))
        greet(device(at_x, at_y, at_z, 1 - core))
        for target in along_x:
            for c in range(2):
                greet(target - core + c)
        for target in along_y:
            greet(target)

    live = (iota((1, LANES), 1) < live_count[0]).astype(F32)
    pen = [penalty_v[f : f + 1, :] for f in range(FACES)]
    pen_sum = pen[0] + pen[1] + pen[2] + pen[3]
    best = jnp.where(live > 0.5, 1.0 + 0.25 * pen_sum, 0.0)
    own_best[...] = best

    def remote(src, dst, send, recv, target):
        return pltpu.make_async_remote_copy(
            src_ref=src,
            dst_ref=dst,
            send_sem=send,
            recv_sem=recv,
            device_id=(target,),
            device_id_type=MESH,
        )

    mine = at_x * column + at_z * 2 + core
    up, up_to = [], []
    for x in range(size_x):
        for c in range(2):
            target = device(x, at_y, 0, c)
            up.append(
                remote(own_best, column_in.at[mine], up_send.at[len(up)], up_recv.at[0], target)
            )
            up_to.append(target != me)

    def count(wanted):
        return sum([each.astype(jnp.int32) for each in wanted])

    partners = count(up_to) + is_head.astype(jnp.int32) * len(along_y)
    partners = partners + count([inside(me + reach) for reach in range(1, REACH + 1)])
    partners = partners + count(
        [
            jnp.logical_and(inside(me - reach), jnp.logical_not(detours(reach)))
            for reach in range(1, REACH + 1)
        ]
    )
    partners = partners + is_detoured.astype(jnp.int32)
    partners = partners + jnp.logical_and(is_head, at_y > 0).astype(jnp.int32) * len(lookouts)
    partners = partners + is_passing.astype(jnp.int32) * (REACH - passed)

    def await_partners():
        pl.semaphore_wait(barrier, partners)

    def send_up():
        for wanted, copy in zip(up_to, up):
            pl.when(wanted)(copy.start)

    @pl.when(jnp.logical_not(is_early))
    def _():
        await_partners()
        send_up()

    for copy in loads:
        copy.wait()

    rows = spread_rows()
    columns = spread_columns()
    inverse = thrice(invert(mass_v[...]))
    square = (FIELD, 3 * FIELD)
    lane_of, row_of = iota(square, 1), iota(square, 0)
    wide = dot(dot(rows, inverse).astype(BF16), columns)
    mass_weights[...] = jnp.where(lane_of % 8 == row_of % 8, wide, 0.0).astype(BF16)

    sends = send_v[0]
    four = jnp.concatenate([sends, sends, sends, sends], axis=1)
    slot_q, slot_group = iota((PEERS, LANES), 0), iota((PEERS, LANES), 1) // SLOTS
    for half in range(2):
        wanted = jnp.zeros((PEERS, LANES), jnp.int32)
        for g in range(4):
            wanted = jnp.where(slot_group == g, ORDER[half * 4 + g], wanted)
        chosen = jnp.sum(jnp.where(slot_q == wanted, four, 0), axis=0, keepdims=True)
        pick = iota((LOCAL, LANES), 0) == chosen
        pick_send[half] = pick.astype(F32).astype(BF16)

    for f in range(FACES):
        lanes = pl.ds(f * LANES, LANES)
        wanted = link_v[f : f + 1, :]
        pick_local[:, lanes] = (iota((LOCAL, LANES), 0) == wanted).astype(F32).astype(BF16)
        for place, q in enumerate(ORDER):
            pick = iota((SLOTS, LANES), 0) + (LOCAL + q * SLOTS) == wanted
            pick_remote[pl.ds(place * SLOTS, SLOTS), lanes] = pick.astype(F32).astype(BF16)

    for place, origin in enumerate(origins):

        @pl.when(jnp.logical_not(inside(origin)))
        def _(place=place):
            for trade in range(2):
                incoming[trade, place] = jnp.zeros((PART, LANES), F32)

    sub = iota((8, LANES), 0)
    scale = jnp.where(sub % 4 == 0, 1.0, 3.0)
    coef = jnp.concatenate(
        [
            jnp.where(
                sub < 4,
                absorption_v[2 * pair : 2 * pair + 1, :],
                absorption_v[2 * pair + 1 : 2 * pair + 2, :],
            )
            * scale
            for pair in range(2)
        ],
        axis=1,
    )
    pen_sum_two = jnp.concatenate([pen_sum, pen_sum], axis=1)
    live_two = jnp.concatenate([live, live], axis=1)
    inv_denom = 1.0 / (coef + 0.5 * pen_sum_two)
    ratio = coef * inv_denom

    for pair in range(2):
        first = source_v[pl.ds(160 * pair, 80), :].reshape(10, 8, LANES)
        other = source_v[pl.ds(160 * pair + 80, 80), :].reshape(10, 8, LANES)
        even, odd = pair_up(first, other)
        lanes = pl.ds(pair * LANES, LANES)
        for p in range(10):
            rhs[2 * p, :, lanes] = even[p] * live
            rhs[2 * p + 1, :, lanes] = odd[p] * live

    def precondition(value, target):
        solved = times(mass_weights[...], value.reshape(FIELD, 2 * LANES))
        target[...] = solved.reshape(NODES, 8, 2 * LANES) * inv_denom[None]

    def fill_table(field):
        high, low = split(field[...])
        for h, part in enumerate((high, low)):
            for pair in range(2):
                block = jnp.concatenate(
                    [
                        jnp.concatenate(
                            [
                                part[FACE_NODE[t][f], :, pair * LANES : (pair + 1) * LANES]
                                for f in range(FACES)
                            ],
                            axis=1,
                        )
                        for t in range(TRI)
                    ],
                    axis=0,
                )
                table[pl.ds(h * ROWS + pair * 80, 80), :] = block.astype(BF16)

    group_of = iota((PART, LANES), 1) // SLOTS

    nearer = (at_z >= size_z // 2).astype(jnp.int32)

    def peer(half, g):
        reach = PEERS // 2 - g
        return jnp.where(half == 0, me - reach, me + reach), jnp.where(half == 0, me + reach, me - reach)

    def trade_copy(trade, half, g):
        place = half * 4 + g
        return remote(
            outgoing.at[trade, place],
            incoming.at[trade, place],
            send_sem.at[trade, place],
            recv_sem.at[trade, place],
            peer(half, g)[0],
        )

    def detour_copy(g):
        return remote(
            outgoing.at[0, g], held.at[g], send_sem.at[0, g], held_recv.at[g], me - column
        )

    def pass_copy(g):
        return remote(
            held.at[g],
            incoming.at[0, g],
            held_send.at[g],
            recv_sem.at[0, g],
            me + column - (REACH - g),
        )

    def pass_on():
        for g in range(REACH):

            @pl.when(passed < REACH - g)
            def _(g=g):
                detour_copy(g).wait_recv()
                pass_copy(g).start()

    def pass_done():
        for g in range(REACH):
            pl.when(passed < REACH - g)(pass_copy(g).wait_send)

    def send_traces(trade):
        for at, half in enumerate((nearer, 1 - nearer)):
            both = dot(table[...], pick_send[half])
            packed = both[:ROWS] + both[ROWS:]
            parts = [packed[j * PART : (j + 1) * PART] for j in range(4)]
            for g in range(4):
                message = None
                for j in range(4):
                    shift = (j - g) * SLOTS % LANES
                    part = pltpu.roll(parts[j], shift, 1) if shift else parts[j]
                    message = part if message is None else jnp.where(group_of == j, part, message)
                outgoing[trade, half * 4 + g] = message
            if trade == 0 and at == 0:
                pl.when(is_early)(await_partners)
                pl.when(is_passing)(pass_on)
            for g in range(4):
                wanted = inside(peer(half, g)[0])
                if trade == 0:
                    detour = jnp.logical_and(half == 0, detours(REACH - g))
                    pl.when(detour)(detour_copy(g).start)
                    wanted = jnp.logical_and(wanted, jnp.logical_not(detour))
                pl.when(wanted)(trade_copy(trade, half, g).start)

    def receive_traces(trade, near):
        for half in (nearer, 1 - nearer):
            for g in range(4):
                pl.when(inside(peer(half, g)[1]))(trade_copy(trade, half, g).wait_recv)
            blocks = []
            for j in range(4):
                gathered = None
                for g in range(4):
                    shift = (g - j) * SLOTS % LANES
                    part = incoming[trade, half * 4 + g]
                    part = pltpu.roll(part, shift, 1) if shift else part
                    gathered = part if gathered is None else jnp.where(group_of == g, part, gathered)
                blocks.append(gathered)
            high, low = split(jnp.concatenate(blocks, axis=0))
            received = jnp.concatenate([high, low], axis=0).astype(BF16)
            both = dot(received, pick_remote[pl.ds(pl.multiple_of(half * LANES, LANES), LANES), :])
            near = near + (both[:ROWS] + both[ROWS:])
        return near

    precondition(rhs[...], direction)
    fill_table(direction)
    send_traces(0)
    pl.when(is_early)(send_up)

    flux = jnp.zeros(square, F32)
    for d in range(3):
        ahead = thrice(stiffness_v[d])
        back = thrice(stiffness_v[d].T)
        from_flux = (row_of % 8) + (d + 1) == lane_of % 8
        from_flux = jnp.logical_and(from_flux, row_of % 4 == 0)
        to_flux = (lane_of % 8) + (d + 1) == row_of % 8
        to_flux = jnp.logical_and(to_flux, lane_of % 4 == 0)
        flux = jnp.where(from_flux, dot(dot(rows, ahead).astype(BF16), columns), flux)
        flux = jnp.where(to_flux, dot(dot(rows, back).astype(BF16), columns), flux)
    flux_weights[...] = flux.astype(BF16)

    geo_in = jnp.where(sub % 4 == 0, 1.0, 0.0)
    geo_out = geo_in
    for d in range(3):
        here = sub % 4 == d + 1
        geo_in = jnp.where(here, geometry_v[d : d + 1, :], geo_in)
        geo_out = jnp.where(here, -geometry_v[d : d + 1, :], geo_out)
    geo_in = jnp.concatenate([geo_in, geo_in], axis=1)
    geo_out = jnp.concatenate([geo_out, geo_out], axis=1)

    pen_node = []
    for node in range(NODES):
        value = None
        for t in range(TRI):
            for f in range(FACES):
                if FACE_NODE[t][f] == node:
                    value = pen[f] if value is None else value + pen[f]
        pen_node.append(jnp.concatenate([value, value], axis=1))
    pen_row = jnp.concatenate(pen, axis=1)
    orient_row = jnp.concatenate([orient_v[f : f + 1, :] for f in range(FACES)], axis=1)

    def apply_local(field):
        both = dot(table[...], pick_local[...])
        value = field[...]
        flux_term = times(flux_weights[...], (value * geo_in[None]).reshape(FIELD, 2 * LANES))
        return both[:ROWS] + both[ROWS:], flux_term.reshape(NODES, 8, 2 * LANES)

    def apply_remote(trade, field, solved, local, target):
        near, flux_term = local
        across = receive_traces(trade, near)
        total = [None] * NODES
        for t in range(TRI):
            sides = []
            for pair in range(2):
                def rows_of(node):
                    start = pair * 80 + node * 8
                    return across[start : start + 8]

                side = rows_of(TURNED[0][t])
                for o in range(1, 6):
                    if TURNED[o][t] != TURNED[0][t]:
                        side = jnp.where(orient_row == o, rows_of(TURNED[o][t]), side)
                sides.append(side * pen_row)
            for f in range(FACES):
                lanes = slice(f * LANES, (f + 1) * LANES)
                jump = jnp.concatenate([side[:, lanes] for side in sides], axis=1)
                node = FACE_NODE[t][f]
                total[node] = jump if total[node] is None else total[node] + jump
        for node in range(NODES):
            value = ratio * solved[node] + geo_out * flux_term[node]
            value = value + pen_node[node] * field[node] - total[node]
            target[node] = live_two * value

    across = []
    for k, y in enumerate(other_y):
        slot = at_y - (at_y > y).astype(jnp.int32)
        target = device(at_x, y, at_z, core)
        across.append(
            remote(level, along_in.at[slot], along_send.at[k], along_recv.at[slot], target)
        )
    ahead_of = [
        remote(
            level, look_in.at[at_y], look_send.at[i], look_recv.at[at_y], device(at_x, 0, z, core)
        )
        for i, z in enumerate(lookouts)
    ]

    def look_out():
        value = None
        for y in range(size_y):
            remote(level, look_in.at[y], look_send.at[0], look_recv.at[y], me + 1 - 2 * core).wait_recv()
            value = look_in[y] if value is None else jnp.maximum(value, look_in[y])
        top[...] = value

    def down(chips):
        return [
            remote(top, top, down_send.at[i], down_recv.at[0], device(at_x, at_y, z, core))
            for i, z in enumerate(z for z in chips if z < size_z)
        ]

    down_to = [
        jnp.logical_or(at_y > 0, z not in lookouts) for z in DOWN if z < size_z
    ]

    def heads_done():
        wait_all(across + ahead_of)
        for wanted, copy in zip(down_to, down(DOWN)):
            pl.when(wanted)(copy.wait_send)

    def meet_column():
        column_in[mine] = own_best[...]
        rest = column_in.at[pl.ds(0, size_x * column - 1)]
        pltpu.make_async_copy(rest, rest, up_recv.at[0]).wait()
        chains = column_in[...].reshape(8, size_x * column // 8, 1, LANES)
        level[...] = jnp.max(jnp.max(chains, axis=0), axis=0)
        if across:
            pl.when(at_y > 0)(across[0].start)
        start_all(ahead_of)
        if across:
            pl.when(at_y == 0)(across[0].start)
        start_all(across[1:])

    def meet_line():
        value = level[...]
        for k in range(size_y - 1):
            remote(level, along_in.at[k], along_send.at[k], along_recv.at[k], me + 1 - 2 * core).wait_recv()
            value = jnp.maximum(value, along_in[k])
        top[...] = value
        for wanted, copy in zip(down_to, down(DOWN)):
            pl.when(wanted)(copy.start)
        write_weights()

    def start_all(copies):
        for copy in copies:
            copy.start()

    def wait_all(copies):
        for copy in copies:
            copy.wait_send()

    def sends_done(trade):
        for place, target in enumerate(targets):
            half, g = divmod(place, 4)
            pl.when(inside(target))(trade_copy(trade, half, g).wait_send)

    def write_weights():
        inv_upper = 1.0 / jnp.max(top[...], axis=1, keepdims=True)
        first_weight = FIRST_WEIGHT * inv_upper
        second_weight = SECOND_WEIGHT * (inv_upper * inv_upper)
        weights_out[0:1, :] = jnp.broadcast_to(first_weight, (1, LANES))
        weights_out[1:2, :] = jnp.broadcast_to(second_weight, (1, LANES))

    def write_out(field, target):
        value = field[...]
        for pair in range(2):
            lanes = slice(pair * LANES, (pair + 1) * LANES)
            for p in range(10):
                even, odd = value[2 * p, :, lanes], value[2 * p + 1, :, lanes]
                low, high = pair_up(even[None], odd[None])
                target[pl.ds(160 * pair + 8 * p, 8), :] = low[0]
                target[pl.ds(160 * pair + 80 + 8 * p, 8), :] = high[0]

    local = apply_local(direction)
    pl.when(is_head)(meet_column)
    apply_remote(0, direction, rhs, local, applied)
    precondition(applied[...], second)
    fill_table(second)
    send_traces(1)
    local = apply_local(second)
    for field, target in (
        (direction, direction_out),
        (second, second_out),
        (rhs, rhs_out),
        (applied, applied_out),
    ):
        write_out(field, target)
    sends_done(0)
    pl.when(is_passing)(pass_done)
    for wanted, copy in zip(up_to, up):
        pl.when(wanted)(copy.wait_send)
    pl.when(is_head)(meet_line)
    apply_remote(1, second, applied, local, twice)
    write_out(twice, twice_out)
    sends_done(1)
    pl.when(is_lookout)(look_out)
    pl.when(jnp.logical_not(jnp.logical_or(is_head, is_lookout)))(down(DOWN)[0].wait_recv)
    for z, chips in RELAY.items():
        pl.when(at_z == z)(functools.partial(start_all, down(chips)))

    pl.when(jnp.logical_not(is_head))(write_weights)
    pl.when(is_head)(heads_done)
    for z, chips in RELAY.items():
        pl.when(at_z == z)(functools.partial(wait_all, down(chips)))


def solution(mesh):
    n = mesh.shape["dom"]
    size_x, size_y, size_z = torus(n)
    along = max(size_y - 1, 1)

    def body(
        source, absorption, geometry, penalty, link, orient, send_index, live_count, mass, stiffness
    ):
        flat = source.transpose(0, 2, 1, 3).reshape(GASES * NODES * COMPS, LANES)
        operands = (
            flat,
            absorption,
            geometry,
            penalty,
            link,
            orient,
            send_index,
            live_count,
            mass,
            stiffness,
        )
        vmem = pltpu.VMEM
        field = vmem((NODES, 8, 2 * LANES), F32)
        dma = pltpu.SemaphoreType.DMA
        hbm = pl.BlockSpec(memory_space=pltpu.HBM)
        first, second, rhs, applied, twice, weights = pl.pallas_call(
            functools.partial(kernel, n),
            out_shape=[jax.ShapeDtypeStruct(flat.shape, F32)] * 5
            + [jax.ShapeDtypeStruct((2, LANES), F32)],
            in_specs=[hbm] * 3
            + [pl.BlockSpec(memory_space=vmem)]
            + [hbm] * 3
            + [pl.BlockSpec(memory_space=pltpu.SMEM)]
            + [hbm] * 2,
            out_specs=[pl.BlockSpec(memory_space=vmem)] * 6,
            scratch_shapes=[
                vmem((320, LANES), F32),
                vmem((4, LANES), F32),
                vmem((3, LANES), F32),
                vmem((4, LANES), jnp.int32),
                vmem((4, LANES), jnp.int32),
                vmem((1, PEERS, SLOTS), jnp.int32),
                vmem((NODES, NODES), F32),
                vmem((3, NODES, NODES), F32),
                field,
                field,
                field,
                field,
                field,
                vmem((FIELD, 3 * FIELD), BF16),
                vmem((FIELD, 3 * FIELD), BF16),
                vmem((2, LOCAL, LANES), BF16),
                vmem((LOCAL, LOCAL), BF16),
                vmem((REMOTE, LOCAL), BF16),
                vmem((2 * ROWS, LOCAL), BF16),
                vmem((2, PEERS, PART, LANES), F32),
                vmem((2, PEERS, PART, LANES), F32),
                vmem((REACH, PART, LANES), F32),
                vmem((1, LANES), F32),
                vmem((2 * size_z * size_x, 1, LANES), F32),
                vmem((along, 1, LANES), F32),
                vmem((size_y, 1, LANES), F32),
                vmem((1, LANES), F32),
                vmem((1, LANES), F32),
                dma((8,)),
                dma((2, PEERS)),
                dma((2, PEERS)),
                dma((REACH,)),
                dma((REACH,)),
                dma((2 * size_x,)),
                dma((1,)),
                dma((along,)),
                dma((along,)),
                dma((len(LOOKOUT),)),
                dma((size_y,)),
                dma((len(DOWN),)),
                dma((1,)),
            ],
            compiler_params=pltpu.CompilerParams(
                collective_id=0, has_side_effects=True, vmem_limit_bytes=32 * 2**20
            ),
            cost_estimate=pl.CostEstimate(
                flops=2_000_000_000, bytes_accessed=1_000_000, transcendentals=0
            ),
        )(*[
                value
                if value is live_count or value is penalty
                else pltpu.with_memory_space_constraint(value, pltpu.HBM)
                for value in operands
            ]
        )
        outs = (
            weights[0] * first + weights[1] * second,
            rhs - weights[0] * applied - weights[1] * twice,
        )
        return tuple(
            out.reshape(GASES, NODES, COMPS, LANES).transpose(0, 2, 1, 3) for out in outs
        )

    in_specs = (
        P(None, None, None, "dom"),
        P(None, "dom"),
        P(None, "dom"),
        P(None, "dom"),
        P(None, "dom"),
        P(None, "dom"),
        P("dom", None, None),
        P("dom"),
        P(),
        P(),
    )
    out_specs = (P(None, None, None, "dom"), P(None, None, None, "dom"))
    return jax.shard_map(body, mesh=mesh, in_specs=in_specs, out_specs=out_specs, check_vma=False)
```
